128 devices in a mesh: clus: 16 (over x, y), col: 8 (over z, core).
Axes of the slice: x: 4, y: 4, z: 4, core: 2. Of those that a mesh axis runs over, the one named last changes fastest.
Arguments:
- density: bfloat16 [8192, 8192], P('clus', 'col'), may hold values from -6 to 6
- dens_pattern: int32 [32, 32], P('clus', 'col'), may hold values 0 or 1
- margin_window: bfloat16 [8192, 4096], P('col', 'clus'), may hold values from -0.0625 to 0.0625
- ovl_pattern: int32 [32, 16], P('col', 'clus'), may hold values 0 or 1
- keep_mask: int32 [16, 16], P('clus', 'col'), may hold values 0 or 1
- basis_values: bfloat16 [32, 256, 4096], P('col'), may hold values from -0.375 to 0.375
- rest_density: float32 [256, 256, 256], P('clus', 'col'), may hold values from -0.6 to 0.6
- slab_owner: int32 [32], replicated, may hold values from 0 to 15
- cell_lengths: float32 [3], replicated, may hold values from 200 to 260
Outputs:
- potential: float32 [256, 256, 256], P('clus', 'col')
- hartree: bfloat16 [8192, 8192], P('clus', 'col')
- product: bfloat16 [4096, 4096], P('clus', 'col')
The draws below stay inside these ranges and needn't reach their ends.
All inputs are finite; a program needn't handle non-finite values. No bound on the sum of `dens_pattern` or of `ovl_pattern` or of `keep_mask` on one device may be relied on, other than what follows from the above.
Results may differ from the reference program's by a relative error of at most 0.0049.
Values may be sent and summed in bfloat16 or wider, within the bound.
A program may use at most 128 MiB of HBM per device.

```python
import math
import jax
import jax.numpy as jnp
import numpy as np
from jax import lax

B = 256
G = 256
BR_DEV = 2
PATCH_Y = 32
QZ = 128
NB = 32
M = 8192
WIN = 4096
PATCH = 4096
N_CLUS = 16
N_COL = 8


def place_ends(result, rng, low, high):
    dims = result.shape
    index_at = [jax.random.randint(jax.random.fold_in(rng, axis), (), 0, dims[axis]) for axis in range(len(dims))]
    result = result.at[tuple(index_at)].set(low)
    longest = dims.index(max(dims))
    index_at[longest] = (index_at[longest] + 1) % dims[longest]
    return result.at[tuple(index_at)].set(high)


def block_levels(rng, extent, split, smallest, high):
    factor_of, own = 1.0, jax.random.fold_in(rng, 6)
    for axis_at, parts in split:
        heights = jnp.exp(jax.random.uniform(jax.random.fold_in(own, axis_at), (parts,), jnp.float32, smallest / len(split), high / len(split)))
        factor_of = factor_of * jnp.repeat(heights, extent[axis_at] // parts).reshape([-1 if axis == axis_at else 1 for axis in range(len(extent))])
    return factor_of


def rank_bounds(count, skew):
    portions = [(1 << 20) // math.isqrt(standing ** skew) + 1 for standing in range(1, count + 1)]
    width = 1 + sum(portions) // (1 << 30)
    return np.cumsum(np.array([max(1, weight // width) for weight in portions]))


def ranked_ids(rng, extent, amount, slope):
    listing = rank_bounds(amount, slope)
    pick = jax.random.randint(jax.random.fold_in(rng, 1), extent, 0, int(listing[amount - 1]))
    grade = jnp.searchsorted(jnp.asarray(listing, jnp.int32), pick, side="right")
    return jax.random.permutation(jax.random.fold_in(rng, 2), amount)[grade].astype(jnp.int32)


def bell_draw(rng, extent, scale, limit, cuts=(), kind=jnp.bfloat16):
    values = scale * jax.random.normal(rng, extent, jnp.float32)
    if cuts:
        values = values * block_levels(rng, extent, cuts, -0.22, 0.18)
    return jnp.clip(values, -limit, limit).astype(kind)


def setup_inputs(seed: int = 0) -> dict:
    key_of = jax.random.split(jax.random.key(seed), 10)
    return {
        "density": bell_draw(key_of[0], (M, M), 1.0, 6.0, ((0, 16), (1, 8))),
        "dens_pattern": place_ends((jax.random.randint(key_of[1], (NB, NB), 0, 2) < 1).astype(jnp.int32), jax.random.fold_in(key_of[1], 1), 0, 1),
        "margin_window": bell_draw(key_of[2], (M, WIN), M ** -0.5, 0.0625, ((0, 8), (1, 16))),
        "ovl_pattern": place_ends((jax.random.randint(key_of[3], (NB, N_CLUS), 0, 2) < 1).astype(jnp.int32), jax.random.fold_in(key_of[3], 1), 0, 1),
        "keep_mask": place_ends((jax.random.randint(key_of[4], (N_CLUS, N_CLUS), 0, 4) < 3).astype(jnp.int32), jax.random.fold_in(key_of[4], 1), 0, 1),
        "basis_values": bell_draw(key_of[5], (NB, B, PATCH), B ** -0.5, 0.375, ((0, 8),)),
        "rest_density": bell_draw(key_of[6], (G, G, G), 0.1, 0.6, ((0, 16), (1, 8)), jnp.float32),
        "slab_owner": place_ends(ranked_ids(key_of[7], (NB,), N_CLUS, 2), jax.random.fold_in(key_of[7], 3), 0, N_CLUS - 1).astype(jnp.int32),
        "cell_lengths": jnp.clip(jax.random.uniform(key_of[8], (3,), jnp.float32, 200.0, 260.0), 200.0, 260.0),
    }


four_pi = 4.0 * math.pi


def green_values(cell_lengths, freq_x, freq_y, freq_z):
    def squared_wave(frequency, axis_pos):
        signed = jnp.where(frequency < G // 2, frequency, frequency - G).astype(jnp.float32)
        scaled = signed * (2.0 * math.pi) / cell_lengths[axis_pos]
        return scaled * scaled

    squared = squared_wave(freq_x, 0) + squared_wave(freq_y, 1) + squared_wave(freq_z, 2)
    at_anchor = (freq_x == 0) & (freq_y == 0) & (freq_z == 0)
    return jnp.where(at_anchor, 0.0, four_pi / jnp.where(at_anchor, 1.0, squared))


def reference(density, dens_pattern, margin_window, ovl_pattern, keep_mask, basis_values, rest_density, slab_owner, cell_lengths):
    masked = (density.reshape(NB, B, NB, B) * dens_pattern.astype(jnp.bfloat16)[:, None, :, None]).reshape(M, M)
    window_rows = masked.reshape(N_CLUS, BR_DEV * B, M)[:, :B].reshape(WIN, M)
    margin_masked = (margin_window.reshape(NB, B, N_CLUS, B) * ovl_pattern.astype(jnp.bfloat16)[:, None, :, None]).reshape(M, WIN)
    summed = jnp.dot(window_rows, margin_masked, preferred_element_type=jnp.float32)
    product = (summed.reshape(N_CLUS, B, N_CLUS, B) * keep_mask.astype(jnp.float32)[:, None, :, None]).reshape(WIN, WIN).astype(jnp.bfloat16)
    phi_stack = basis_values.reshape(M, PATCH)
    lifted = jnp.dot(masked, phi_stack, preferred_element_type=jnp.float32)
    patch_rho = jnp.sum(basis_values.astype(jnp.float32) * lifted.reshape(NB, B, PATCH), axis=1)
    block_ids = jnp.arange(NB, dtype=jnp.int32)
    plane_count = G // N_CLUS
    line_count = G // N_COL
    lines_dev = PATCH_Y // N_COL
    x_cells = slab_owner.astype(jnp.int32) * plane_count + block_ids % plane_count
    col_lines = jnp.arange(N_COL, dtype=jnp.int32)[:, None] * line_count + jnp.arange(lines_dev, dtype=jnp.int32)[None, :]
    y_cells = col_lines[None, :, :] + ((block_ids // plane_count) * lines_dev)[:, None, None]
    z_cells = (G - QZ) // 2 + jnp.arange(QZ, dtype=jnp.int32)
    index_x = x_cells[:, None, None, None]
    index_y = y_cells[:, :, :, None]
    index_z = z_cells[None, None, None, :]
    placed = jnp.zeros((G, G, G), jnp.float32).at[index_x, index_y, index_z].add(patch_rho.reshape(NB, N_COL, lines_dev, QZ))
    density_grid = rest_density + placed
    frequency = jnp.arange(G, dtype=jnp.int32)
    green_table = green_values(cell_lengths, frequency[:, None, None], frequency[None, :, None], frequency[None, None, :])
    spectrum = jnp.fft.fftn(density_grid) * green_table
    potential = jnp.real(jnp.fft.ifftn(spectrum)).astype(jnp.float32)
    patch_pot = potential[index_x, index_y, index_z].reshape(NB, PATCH)
    weighted = (basis_values.astype(jnp.float32) * patch_pot[:, None, :]).astype(jnp.bfloat16)
    pattern_float = dens_pattern.astype(jnp.float32)

    def one_row(inputs):
        rows_bf, pattern_row = inputs
        full_row = lax.dot_general(rows_bf, phi_stack, (((1,), (1,)), ((), ())), preferred_element_type=jnp.float32)
        return (full_row.reshape(B, NB, B) * pattern_row[None, :, None]).reshape(B, M).astype(jnp.bfloat16)

    hartree = lax.map(one_row, (weighted, pattern_float)).reshape(M, M)
    return potential, hartree, product
```

```python
import functools
import math

import jax
import jax.numpy as jnp
import ml_dtypes
import numpy as np
from jax import lax
from jax.experimental import pallas as pl
from jax.experimental.pallas import tpu as pltpu
from jax.sharding import PartitionSpec as P

B = 256
G = 256
QZ = 128
NX, NY, NZ = 4, 4, 4
ND = 128
CH = 512
four_pi = 4.0 * math.pi
f32 = jnp.float32
bf16 = jnp.bfloat16
MESH = pl.DeviceIdType.MESH
NT = (((1,), (1,)), ((), ()))
TN = (((0,), (0,)), ((), ()))
NN = (((1,), (0,)), ((), ()))


def split_np(a):
    hi = a.astype(np.float32).astype(ml_dtypes.bfloat16)
    lo = (a - hi.astype(np.float64)).astype(np.float32).astype(ml_dtypes.bfloat16)
    return [hi, lo]


def x_of_row(row):
    return (row % 64) // 4 * 16 + row % 4 * 4 + row // 64


@functools.lru_cache(maxsize=1)
def tables():
    n = np.arange(G)
    ang = 2.0 * np.pi * (n[:, None] * n[None, :] % G) / G
    cos, sin = np.cos(ang), np.sin(ang)
    half = cos[:128], sin[:128]
    tz = np.concatenate([half[0], -half[1]], 0)
    tz[128] = cos[128]
    tzi = np.concatenate([2.0 * half[0], -2.0 * half[1]], 0)
    tzi[0] = 1.0
    tzi[128] = cos[128]
    tzi = tzi / float(G) ** 3
    perm = x_of_row(n)
    wx = np.concatenate([cos[:, perm], sin[:, perm]], 0)
    wi = np.concatenate([cos[perm], sin[perm]], 0)
    tp = np.concatenate([tzi[:128, 64:192], tzi[128:, 64:192]], 1)
    row = np.arange(1024)
    c, l, il, j = row // 64, row // 8 % 8, row // 4 % 2, row % 4
    y = l * 32 + (2 * c + il) // 16 * 4 + j
    sel_y = (y[:, None] == n[None, :]).astype(np.float64)
    sel_y = [sel_y.astype(np.float32).astype(ml_dtypes.bfloat16)]
    t1 = np.concatenate(split_np(tz) + split_np(tzi) + split_np(wx) + split_np(wi) + split_np(tp) + sel_y, 0)
    ty = np.concatenate(split_np(np.concatenate([cos, sin], 1)), 0)
    ri, il, y = row // 512, row // 256 % 2, row % 256
    lane = ri * 64 + il * 32 + y // 32 * 4 + y % 4
    sel_c = (lane[:, None] == np.arange(128)[None, :]) & (y % 32 < 8)[:, None]
    sel_c = sel_c.astype(np.float32).astype(ml_dtypes.bfloat16)
    tzp = np.zeros((ND, 8, 128), np.float32)
    tzp[:, 0] = tz[:128, 64:192]
    tzp[:, 1] = tz[128:, 64:192]
    return t1, ty, sel_c, tzp


ROWS = {}
at = 0
for name, rows in (
    ("tz", 256), ("tzi", 256), ("wx", 512), ("wi", 512), ("tp", 128)
):
    ROWS[name] = (at, rows)
    at += 2 * rows
ROWS["sel_y"] = (at, 1024)
T1_ROWS = at + 1024


def split2(a):
    hi = a.astype(bf16)
    lo = (a - hi.astype(f32)).astype(bf16)
    return hi, lo


def dot(a, b, dims=NN):
    return lax.dot_general(a, b, dims, preferred_element_type=f32)


def dot3(a, b, dims=NN):
    return dot(a[0], b[0], dims) + (dot(a[0], b[1], dims) + dot(a[1], b[0], dims))


def kernel(
    pat_ref, len_ref, dens_ref, phi_ref, rest_ref, xcell_ref, own_ref,
    t1_hbm, ty_hbm, selc_hbm, tzp_hbm,
    pot_ref, har_ref,
    phi, rblk, relay, masked, wt, t1, ty, selc, tzp,
    s1, r1, s2, r2, s3, r3, rp, rq, rho, rg, xa, ga, gb, big,
    lsem, tsem, rsem, ssem, a_s, a_r, q_s, q_r, g_s, g_r, p_s, p_r, b_s, b_r,
):
    c = lax.axis_index("clus")
    k = lax.axis_index("col")
    me = c * 8 + k
    x, y = c // 4, c % 4
    z, h = k // 2, k % 2
    zp, zm, z2 = (z + 1) % 4, (z + 3) % 4, (z + 2) % 4
    root = h == y // 2
    hub = x == z
    far = jnp.logical_not(hub)
    twin = (c, z * 2 + 1 - h)

    def part(name, lo):
        first, rows = ROWS[name]
        return t1[pl.ds(first + lo * rows, rows), :]

    def table(name):
        return part(name, 0), part(name, 1)

    def local(src, dst, sem):
        return pltpu.make_async_copy(src, dst, sem)

    def remote(src, dst, send, recv, to):
        return pltpu.make_async_remote_copy(
            src_ref=src, dst_ref=dst, send_sem=send, recv_sem=recv, device_id=to, device_id_type=MESH
        )

    def others(fn):
        def body(i, carry):
            p = lax.rem(me + i, ND)
            fn(p, (p // 8, p % 8))
            return carry

        lax.fori_loop(1, ND, body, 0)

    bar = pltpu.get_barrier_semaphore()
    others(lambda p, to: pl.semaphore_signal(bar, inc=1, device_id=to, device_id_type=MESH))
    loads = [
        local(t1_hbm, t1, lsem.at[0]),
        local(phi_ref, phi, lsem.at[1]),
        local(ty_hbm, ty, lsem.at[2]),
        local(selc_hbm, selc, lsem.at[3]),
        local(tzp_hbm.at[me], tzp, lsem.at[4]),
    ]
    for copy in loads:
        copy.start()
    for i in range(2):
        for j in range(4):
            keep = pat_ref[i, j].astype(f32).astype(bf16)
            at_rows, at_cols = pl.ds(i * B, B), pl.ds(j * B, B)
            masked[at_rows, at_cols] = dens_ref[at_rows, at_cols] * keep
    loads[0].wait()
    lines = dot3(table("tz"), split2(rest_ref[...]), NT)
    for i in range(2):
        for j in range(4):
            s1[:, i * 4 + j, :] = lines[i * 128 : (i + 1) * 128, j * 128 : (j + 1) * 128]
    loads[1].wait()
    pl.semaphore_wait(bar, ND - 1)

    first = 2 * (y % 2)

    def own_part(l):
        return phi.at[pl.ds(first, 2), :, pl.ds(pl.multiple_of(l * CH, CH), CH)]

    to_send = []

    def send(when, src, dst, recv, to):
        index = len(to_send)
        copy = remote(src, dst, ssem.at[index], recv, to)
        to_send.append((when, copy))
        pl.when(when)(copy.start)

    for up, half in ((True, 0), (False, 1), (True, 1), (False, 0)):
        slot = 0 if up else 1
        send(
            root, own_part(2 * x + half), relay.at[slot], tsem.at[slot],
            (c, (zp if up else zm) * 2 + half),
        )
    hub_root = jnp.logical_and(hub, root)
    for l in range(8):
        send(hub_root, own_part(l), rblk.at[l], rsem.at[l], twin)

        @pl.when(hub_root)
        def _():
            local(own_part(l), rblk.at[l], rsem.at[l]).start()

    others(lambda p, to: remote(s1.at[p], r1.at[c, k], a_s, a_r, to).start())
    local(s1.at[me], r1.at[c, k], a_r).start()

    mine = 2 * x + h
    for slot, plane in ((0, zm), (1, zp), (2, z2)):
        local(relay.at[slot], relay.at[slot], tsem.at[slot]).wait()
        if slot == 0:
            send(h == 0, relay.at[0], relay.at[2], tsem.at[2], (c, zp * 2))
        if slot == 1:
            send(h == 1, relay.at[1], relay.at[2], tsem.at[2], (c, zm * 2 + 1))
        here = plane == x
        send(here, relay.at[slot], rblk.at[mine], rsem.at[mine], twin)
        send(jnp.logical_not(here), relay.at[slot], rblk.at[mine], rsem.at[mine], (plane * 4 + y, k))

        @pl.when(here)
        def _():
            local(relay.at[slot], rblk.at[mine], rsem.at[mine]).start()

    row_id = lax.broadcasted_iota(jnp.int32, (G, G), 0)
    col_id = lax.broadcasted_iota(jnp.int32, (G, G), 1)

    def wave(freq, axis):
        signed = jnp.where(freq < G // 2, freq, freq - G).astype(f32)
        scaled = signed * (2.0 * math.pi) / jnp.full(freq.shape, len_ref[axis], f32)
        return scaled * scaled

    flat = wave(row_id, 0) + wave(col_id, 1)
    for out, kz in ((ga, me), (gb, jnp.where(me == 0, 128, me))):
        kz = jnp.full((G, G), kz, jnp.int32)
        anchor = (row_id == 0) & (col_id == 0) & (kz == 0)
        out[...] = jnp.where(anchor, 0.0, four_pi / jnp.where(anchor, 1.0, flat + wave(kz, 2)))

    fwd = 25

    def step(t, carry):
        own = (t == 0) | ((t % 2 == 1) & (t < 7))
        dx = jnp.where(own, (t + 1) // 2, jnp.where(t == 7, 3, t // 2 - 1))
        l = 2 * ((x + dx) % 4) + jnp.where(own, h, 1 - h)
        local(rblk.at[l], rblk.at[l], rsem.at[l]).wait()

        @pl.when(own & (dx > 0) & far)
        def _():
            remote(rblk.at[l], rblk.at[l], ssem.at[fwd + dx], rsem.at[l], twin).start()

        cells = pl.ds(pl.multiple_of(l * CH, CH), CH)
        values = phi[:, :, cells].reshape(4 * B, CH)
        for i in range(2):
            lifted = dot(masked[i * B : (i + 1) * B, :], values)
            summed = jnp.sum(rblk[l, i].astype(f32) * lifted, axis=0, keepdims=True)
            for j in range(4):
                rp[l, pl.ds(i * 4 + j, 1), :] = summed[:, j * 128 : (j + 1) * 128]
        away = l != k

        @pl.when(away)
        def _():
            remote(rp.at[l], rq.at[k], q_s.at[l], q_r.at[k], (c, l)).start()

        @pl.when(jnp.logical_not(away))
        def _():
            local(rp.at[l], rq.at[k], q_r.at[k]).start()

        return carry

    lax.fori_loop(0, 8, step, 0)
    for l in range(8):
        local(rq.at[l], rq.at[l], q_r.at[l]).wait()
    rho[...] = jnp.sum(rq[...], axis=0)

    others(lambda p, to: remote(rho, rg.at[me], g_s, g_r, to).start())
    local(rho, rg.at[me], g_r).start()

    lane = lax.broadcasted_iota(jnp.int32, (1, 1, 128), 2) // 32
    low = lax.broadcasted_iota(jnp.int32, (1, 8, 1), 1) < 4
    local(r1, r1, a_r).wait()
    for kk in range(2):
        got = [r1[:, kk * 4 + k4] for k4 in range(4)]
        for p4 in range(4):
            tile = got[p4]
            for k4 in range(4):
                if k4 != p4:
                    turned = pltpu.roll(got[k4], (k4 - p4) % 4 * 32, 2)
                    tile = jnp.where(lane == k4, turned, tile)
            pairs = tile.reshape(8, 2, 8, 128)
            even, odd = pairs[:, 0], pairs[:, 1]
            at_rows, at_cols = pl.ds(p4 * 64, 64), pl.ds(kk * 128, 128)
            xa[at_rows, at_cols] = jnp.where(low, even, pltpu.roll(odd, 4, 1)).reshape(64, 128)
            xa[pl.ds(256 + p4 * 64, 64), at_cols] = jnp.where(low, pltpu.roll(even, 4, 1), odd).reshape(64, 128)

    for copy in loads[2:]:
        copy.wait()
    row_x = x_of_row(lax.broadcasted_iota(jnp.int32, (G, 1), 0))
    sits = row_x == xcell_ref[...]
    local(rg, rg, g_r).wait()
    coef = lax.dot_general(
        tzp[...], rg[...].reshape(8 * ND, QZ), NT,
        precision=lax.Precision.HIGHEST, preferred_element_type=f32,
    )
    sel_first, sel_rows = ROWS["sel_y"]
    sel_y = t1[pl.ds(sel_first, sel_rows), :]
    for i in range(2):
        add = None
        for piece in split2(coef[i : i + 1, :]):
            placed = jnp.where(sits, piece.astype(f32), 0.0).astype(bf16)
            term = dot(placed, sel_y)
            add = term if add is None else add + term
        xa[pl.ds(i * G, G), :] = xa[pl.ds(i * G, G), :] + add

    ty_pair = ty[0:G, :], ty[G : 2 * G, :]
    big[...] = dot3(split2(xa[...]), ty_pair)
    wx = table("wx")
    fields = []
    for i in range(2):
        quad = dot3(wx, split2(big[pl.ds(i * G, G), :]))
        fields.append((quad[:G, :G] - quad[G:, G:], -(quad[G:, :G] + quad[:G, G:])))
    (a_re, a_im), (b_re, b_im) = fields
    xa[0:G, :] = ga[...] * a_re - gb[...] * b_im
    xa[G : 2 * G, :] = ga[...] * a_im + gb[...] * b_re
    back = dot3(split2(xa[...]), ty_pair)
    big[0:G, 0:G] = back[:G, :G] - back[G:, G:]
    big[0:G, G : 2 * G] = back[:G, G:] + back[G:, :G]
    quad = dot3(table("wi"), split2(big[0:G, :]))
    xa[0:G, :] = quad[:G, :G] - quad[G:, G:]
    xa[G : 2 * G, :] = quad[:G, G:] + quad[G:, :G]

    order = lax.broadcasted_iota(jnp.int32, (32, G), 0)
    block = order % 16 * 2 + order // 16
    row_of = x_of_row(lax.broadcasted_iota(jnp.int32, (32, G), 1))
    pick = (row_of == own_ref[...] * 16 + block % 16).astype(f32).astype(bf16)
    line = lax.broadcasted_iota(jnp.int32, (32, G), 1)
    valid = line % 32 // 4 == block // 16
    rows = []
    for i in range(2):
        hi, lo = split2(xa[pl.ds(i * G, G), :])
        here = jnp.where(valid, dot(pick, hi) + dot(pick, lo), 0.0)
        rows += [here[0:16], here[16:32]]
    hi, lo = split2(jnp.concatenate(rows, axis=1))
    packed = dot(hi, selc[...]) + dot(lo, selc[...])
    for i in range(16):
        s3[i] = packed[i : i + 1, :]
    others(lambda p, to: remote(s3.at[p // 8], r3.at[me], p_s, p_r, to).start())
    local(s3.at[c], r3.at[me], p_r).start()

    for kk in range(2):
        tiles = []
        at_cols = pl.ds(kk * 128, 128)
        for p4 in range(4):
            re = xa[pl.ds(p4 * 64, 64), at_cols].reshape(8, 8, 128)
            im = xa[pl.ds(256 + p4 * 64, 64), at_cols].reshape(8, 8, 128)
            even = jnp.where(low, re, pltpu.roll(im, 4, 1))
            odd = jnp.where(low, pltpu.roll(re, 4, 1), im)
            tiles.append(jnp.stack([even, odd], axis=1).reshape(16, 8, 128))
        for k4 in range(4):
            tile = tiles[k4]
            for p4 in range(4):
                if p4 != k4:
                    tile = jnp.where(lane == p4, pltpu.roll(tiles[p4], (p4 - k4) % 4 * 32, 2), tile)
            s2[:, kk * 4 + k4] = tile
    others(lambda p, to: remote(s2.at[p // 8, p % 8], r2.at[me], b_s, b_r, to).start())
    local(s2.at[c, k], r2.at[me], b_r).start()

    local(r3, r3, p_r).wait()
    arrived = split2(r3[...].reshape(ND, 128))
    both = dot3(arrived, table("tp"), TN)
    rho_pot = both[:64, :128] + both[64:, 128:]
    for i in range(2):
        for l in range(8):
            for j in range(4):
                at_row = i * 32 + l * 4 + j
                scaled = rblk[l, i, :, pl.ds(j * 128, 128)].astype(f32) * rho_pot[at_row : at_row + 1, :]
                wt[pl.ds(i * B, B), pl.ds(l * CH + j * 128, 128)] = scaled.astype(bf16)
    for j in range(4):
        for i in range(2):
            block_sum = dot(wt[pl.ds(i * B, B), :], phi[j], NT)
            har_ref[pl.ds(i * B, B), pl.ds(j * B, B)] = (block_sum * pat_ref[i, j].astype(f32)).astype(bf16)

    local(r2, r2, b_r).wait()
    tzi = table("tzi")
    for j in range(4):
        got = jnp.concatenate([r2[:, j, :], r2[:, 4 + j, :]], axis=0)
        pot_ref[pl.ds(j * 128, 128), :] = dot3(split2(got), tzi, TN)

    for when, copy in to_send:
        pl.when(when)(copy.wait_send)
    for dx in range(1, 4):
        l = 2 * ((x + dx) % 4) + h

        @pl.when(far)
        def _():
            remote(rblk.at[l], rblk.at[l], ssem.at[fwd + dx], rsem.at[l], twin).wait_send()

    for l in range(8):

        @pl.when(l != k)
        def _():
            remote(rp.at[l], rq.at[k], q_s.at[l], q_r.at[k], (c, l)).wait_send()

    most = pl.ds(0, ND - 1)
    for src, sem in ((s1, a_s), (rg, g_s), (r3, p_s), (r2, b_s)):
        local(src.at[most], src.at[most], sem).wait()


def main_call(density, pattern, basis, rest, slab_owner, lengths):
    t1, ty, selc, tzp = tables()
    blocks = jnp.arange(32, dtype=jnp.int32)
    x_cells = slab_owner * 16 + blocks % 16
    xcell = jnp.broadcast_to(x_cells.reshape(16, 1, 2, 1), (16, 8, 2, 4)).reshape(1, 1024)
    order = slab_owner.reshape(16, 2).T.reshape(32, 1)
    vmem = pl.BlockSpec(memory_space=pltpu.VMEM)
    smem = pl.BlockSpec(memory_space=pltpu.SMEM)
    hbm = pl.BlockSpec(memory_space=pl.ANY)
    V = pltpu.VMEM
    D = pltpu.SemaphoreType.DMA
    return pl.pallas_call(
        kernel,
        out_shape=(
            jax.ShapeDtypeStruct((512, G), f32),
            jax.ShapeDtypeStruct((512, 1024), bf16),
        ),
        in_specs=[smem, smem, vmem, hbm, vmem, vmem, vmem, hbm, hbm, hbm, hbm],
        out_specs=(vmem, vmem),
        scratch_shapes=[
            V((4, B, 4096), bf16),
            V((8, 2, B, CH), bf16),
            V((3, 2, B, CH), bf16),
            V((512, 1024), bf16),
            V((512, 4096), bf16),
            V((T1_ROWS, G), bf16),
            V((2 * G, 2 * G), bf16),
            V((1024, 128), bf16),
            V((8, 128), f32),
            V((ND, 8, 128), f32),
            V((16, 8, 8, 128), f32),
            V((16, 8, 8, 128), f32),
            V((ND, 8, 128), f32),
            V((16, 1, 128), f32),
            V((ND, 1, 128), f32),
            V((8, 8, 128), f32),
            V((8, 8, 128), f32),
            V((8, 128), f32),
            V((ND, 8, 128), f32),
            V((2 * G, G), f32),
            V((G, G), f32),
            V((G, G), f32),
            V((2 * G, 2 * G), f32),
            D((5,)),
            D((3,)),
            D((8,)),
            D((32,)),
            D(()),
            D(()),
            D((8,)),
            D((8,)),
            D(()),
            D(()),
            D(()),
            D(()),
            D(()),
            D(()),
        ],
        compiler_params=pltpu.CompilerParams(
            collective_id=0, has_side_effects=True, vmem_limit_bytes=56 << 20
        ),
        cost_estimate=pl.CostEstimate(flops=12 * 10**9, bytes_accessed=24 << 20, transcendentals=0),
    )(pattern, lengths, density, basis, rest, xcell, order, t1, ty, selc, tzp)


def per_device(
    density, dens_pattern, margin_window, ovl_pattern, keep_mask, basis_values, rest_density,
    slab_owner, cell_lengths,
):
    clus_count = lax.axis_size("clus")
    col_count = lax.axis_size("col")
    ratio_cols = clus_count // col_count
    window_rows = (
        density[:B].reshape(B, 4, B) * dens_pattern[0].astype(bf16)[None, :, None]
    ).reshape(B, 4 * B)
    margin_masked = (
        margin_window.reshape(4, B, B) * ovl_pattern.astype(bf16)[:, :, None]
    ).reshape(4 * B, B)
    partial_sums = jnp.dot(
        window_rows, lax.all_gather(margin_masked, "clus", axis=1, tiled=True), preferred_element_type=f32
    )
    summed = lax.psum_scatter(partial_sums, "col", scatter_dimension=1, tiled=True)
    product = (
        (summed.reshape(B, ratio_cols, B) * keep_mask.astype(f32)[0][None, :, None])
        .reshape(B, ratio_cols * B)
        .astype(bf16)
    )
    potential, hartree = main_call(
        density, dens_pattern, basis_values, rest_density.reshape(512, G), slab_owner, cell_lengths
    )
    return potential.reshape(16, 32, G), hartree, product


def solution(mesh):
    return jax.shard_map(
        per_device,
        mesh=mesh,
        in_specs=(
            P("clus", "col"),
            P("clus", "col"),
            P("col", "clus"),
            P("col", "clus"),
            P("clus", "col"),
            P("col", None, None),
            P("clus", "col", None),
            P(),
            P(),
        ),
        out_specs=(P("clus", "col", None), P("clus", "col"), P("clus", "col")),
        check_vma=False,
    )
```

```python
import functools
import math

import jax
import jax.numpy as jnp
import ml_dtypes
import numpy as np
from jax import lax
from jax.experimental import pallas as pl
from jax.experimental.pallas import tpu as pltpu
from jax.sharding import PartitionSpec as P

B = 256
G = 256
QZ = 128
NX, NY, NZ = 4, 4, 4
ND = 128
CH = 512
four_pi = 4.0 * math.pi
f32 = jnp.float32
bf16 = jnp.bfloat16
MESH = pl.DeviceIdType.MESH
NT = (((1,), (1,)), ((), ()))
TN = (((0,), (0,)), ((), ()))
NN = (((1,), (0,)), ((), ()))


def split_np(a):
    hi = a.astype(np.float32).astype(ml_dtypes.bfloat16)
    lo = (a - hi.astype(np.float64)).astype(np.float32).astype(ml_dtypes.bfloat16)
    return [hi, lo]


def x_of_row(row):
    return (row % 64) // 4 * 16 + row % 4 * 4 + row // 64


@functools.lru_cache(maxsize=1)
def tables():
    n = np.arange(G)
    ang = 2.0 * np.pi * (n[:, None] * n[None, :] % G) / G
    cos, sin = np.cos(ang), np.sin(ang)
    half = cos[:128], sin[:128]
    tz = np.concatenate([half[0], -half[1]], 0)
    tz[128] = cos[128]
    tzi = np.concatenate([2.0 * half[0], -2.0 * half[1]], 0)
    tzi[0] = 1.0
    tzi[128] = cos[128]
    tzi = tzi / float(G) ** 3
    perm = x_of_row(n)
    wx = np.concatenate([cos[:, perm], sin[:, perm]], 0)
    wi = np.concatenate([cos[perm], sin[perm]], 0)
    tp = np.concatenate([tzi[:128, 64:192], tzi[128:, 64:192]], 1)
    row = np.arange(1024)
    c, l, il, j = row // 64, row // 8 % 8, row // 4 % 2, row % 4
    y = l * 32 + (2 * c + il) // 16 * 4 + j
    sel_y = (y[:, None] == n[None, :]).astype(np.float64)
    sel_y = [sel_y.astype(np.float32).astype(ml_dtypes.bfloat16)]
    t1 = np.concatenate(split_np(tz) + split_np(tzi) + split_np(wx) + split_np(wi) + split_np(tp) + sel_y, 0)
    ty = np.concatenate(split_np(np.concatenate([cos, sin], 1)), 0)
    ri, il, y = row // 512, row // 256 % 2, row % 256
    lane = ri * 64 + il * 32 + y // 32 * 4 + y % 4
    sel_c = (lane[:, None] == np.arange(128)[None, :]) & (y % 32 < 8)[:, None]
    sel_c = sel_c.astype(np.float32).astype(ml_dtypes.bfloat16)
    tzp = np.zeros((ND, 8, 128), np.float32)
    tzp[:, 0] = tz[:128, 64:192]
    tzp[:, 1] = tz[128:, 64:192]
    return t1, ty, sel_c, tzp


ROWS = {}
at = 0
for name, rows in (
    ("tz", 256), ("tzi", 256), ("wx", 512), ("wi", 512), ("tp", 128)
):
    ROWS[name] = (at, rows)
    at += 2 * rows
ROWS["sel_y"] = (at, 1024)
T1_ROWS = at + 1024


def split2(a):
    hi = a.astype(bf16)
    lo = (a - hi.astype(f32)).astype(bf16)
    return hi, lo


def dot(a, b, dims=NN):
    return lax.dot_general(a, b, dims, preferred_element_type=f32)


def dot3(a, b, dims=NN):
    return dot(a[0], b[0], dims) + (dot(a[0], b[1], dims) + dot(a[1], b[0], dims))


def kernel(
    pat_ref, len_ref, ovl_ref, keep_ref, margin_ref, dens_ref, phi_ref, rest_ref, xcell_ref, own_ref,
    t1_hbm, ty_hbm, selc_hbm, tzp_hbm,
    pot_ref, har_ref, prod_ref,
    phi, rblk, relay, masked, wt, t1, ty, selc, tzp,
    s1, r1, s2, r2, s3, r3, rp, rq, rho, rg, xa, ga, gb, big,
    wd, wm, tt, trx, zs, zr, ys, yr,
    lsem, tsem, rsem, ssem, a_s, a_r, q_s, q_r, g_s, g_r, p_s, p_r, b_s, b_r,
    wd_s, wd_r, wm_s, wm_r, tw_s, tw_r, zs_s, zr_r, ys_s, yr_r,
):
    c = lax.axis_index("clus")
    k = lax.axis_index("col")
    me = c * 8 + k
    x, y = c // 4, c % 4
    z, h = k // 2, k % 2
    zp, zm, z2 = (z + 1) % 4, (z + 3) % 4, (z + 2) % 4
    root = h == y // 2
    hub = x == z
    far = jnp.logical_not(hub)
    twin = (c, z * 2 + 1 - h)

    def part(name, lo):
        first, rows = ROWS[name]
        return t1[pl.ds(first + lo * rows, rows), :]

    def table(name):
        return part(name, 0), part(name, 1)

    def local(src, dst, sem):
        return pltpu.make_async_copy(src, dst, sem)

    def remote(src, dst, send, recv, to):
        return pltpu.make_async_remote_copy(
            src_ref=src, dst_ref=dst, send_sem=send, recv_sem=recv, device_id=to, device_id_type=MESH
        )

    def others(fn):
        def body(i, carry):
            p = lax.rem(me + i, ND)
            fn(p, (p // 8, p % 8))
            return carry

        lax.fori_loop(1, ND, body, 0)

    bar = pltpu.get_barrier_semaphore()
    others(lambda p, to: pl.semaphore_signal(bar, inc=1, device_id=to, device_id_type=MESH))
    loads = [
        local(t1_hbm, t1, lsem.at[0]),
        local(phi_ref, phi, lsem.at[1]),
        local(ty_hbm, ty, lsem.at[2]),
        local(selc_hbm, selc, lsem.at[3]),
        local(tzp_hbm.at[me], tzp, lsem.at[4]),
    ]
    for copy in loads:
        copy.start()
    for i in range(2):
        for j in range(4):
            keep = pat_ref[i, j].astype(f32).astype(bf16)
            at_rows, at_cols = pl.ds(i * B, B), pl.ds(j * B, B)
            masked[at_rows, at_cols] = dens_ref[at_rows, at_cols] * keep
    wd[y] = masked[0:B, :]
    for j in range(4):
        at_rows = pl.ds(j * B, B)
        wm[x, at_rows, :] = margin_ref[at_rows, :] * ovl_ref[j, 0].astype(f32).astype(bf16)
    loads[0].wait()
    lines = dot3(table("tz"), split2(rest_ref[...]), NT)
    for i in range(2):
        for j in range(4):
            s1[:, i * 4 + j, :] = lines[i * 128 : (i + 1) * 128, j * 128 : (j + 1) * 128]
    loads[1].wait()
    pl.semaphore_wait(bar, ND - 1)

    to_y = [(x * 4 + (y + i) % 4, k) for i in range(1, 4)]
    to_x = [((x + i) % 4 * 4 + y, k) for i in range(1, 4)]
    rows_out = [remote(wd.at[y], wd.at[y], wd_s.at[i], wd_r.at[y], to) for i, to in enumerate(to_y)]
    cols_out = [remote(wm.at[x], wm.at[x], wm_s.at[i], wm_r.at[x], to) for i, to in enumerate(to_x)]
    for copy in rows_out:
        copy.start()

    first = 2 * (y % 2)

    def own_part(l):
        return phi.at[pl.ds(first, 2), :, pl.ds(pl.multiple_of(l * CH, CH), CH)]

    to_send = []

    def send(when, src, dst, recv, to):
        index = len(to_send)
        copy = remote(src, dst, ssem.at[index], recv, to)
        to_send.append((when, copy))
        pl.when(when)(copy.start)

    for up, half in ((True, 0), (False, 1), (True, 1), (False, 0)):
        slot = 0 if up else 1
        send(
            root, own_part(2 * x + half), relay.at[slot], tsem.at[slot],
            (c, (zp if up else zm) * 2 + half),
        )
    hub_root = jnp.logical_and(hub, root)
    for l in range(8):
        send(hub_root, own_part(l), rblk.at[l], rsem.at[l], twin)

        @pl.when(hub_root)
        def _():
            local(own_part(l), rblk.at[l], rsem.at[l]).start()

    for copy in cols_out:
        copy.start()

    others(lambda p, to: remote(s1.at[p], r1.at[c, k], a_s, a_r, to).start())
    local(s1.at[me], r1.at[c, k], a_r).start()

    mine = 2 * x + h
    for slot, plane in ((0, zm), (1, zp), (2, z2)):
        local(relay.at[slot], relay.at[slot], tsem.at[slot]).wait()
        if slot == 0:
            send(h == 0, relay.at[0], relay.at[2], tsem.at[2], (c, zp * 2))
        if slot == 1:
            send(h == 1, relay.at[1], relay.at[2], tsem.at[2], (c, zm * 2 + 1))
        here = plane == x
        send(here, relay.at[slot], rblk.at[mine], rsem.at[mine], twin)
        send(jnp.logical_not(here), relay.at[slot], rblk.at[mine], rsem.at[mine], (plane * 4 + y, k))

        @pl.when(here)
        def _():
            local(relay.at[slot], rblk.at[mine], rsem.at[mine]).start()

    row_id = lax.broadcasted_iota(jnp.int32, (G, G), 0)
    col_id = lax.broadcasted_iota(jnp.int32, (G, G), 1)

    def wave(freq, axis):
        signed = jnp.where(freq < G // 2, freq, freq - G).astype(f32)
        scaled = signed * (2.0 * math.pi) / jnp.full(freq.shape, len_ref[axis], f32)
        return scaled * scaled

    flat = wave(row_id, 0) + wave(col_id, 1)
    for out, kz in ((ga, me), (gb, jnp.where(me == 0, 128, me))):
        kz = jnp.full((G, G), kz, jnp.int32)
        anchor = (row_id == 0) & (col_id == 0) & (kz == 0)
        out[...] = jnp.where(anchor, 0.0, four_pi / jnp.where(anchor, 1.0, flat + wave(kz, 2)))

    fwd = 25

    def step(t, carry):
        own = (t == 0) | ((t % 2 == 1) & (t < 7))
        dx = jnp.where(own, (t + 1) // 2, jnp.where(t == 7, 3, t // 2 - 1))
        l = 2 * ((x + dx) % 4) + jnp.where(own, h, 1 - h)
        local(rblk.at[l], rblk.at[l], rsem.at[l]).wait()

        @pl.when(own & (dx > 0) & far)
        def _():
            remote(rblk.at[l], rblk.at[l], ssem.at[fwd + dx], rsem.at[l], twin).start()

        cells = pl.ds(pl.multiple_of(l * CH, CH), CH)
        values = phi[:, :, cells].reshape(4 * B, CH)
        for i in range(2):
            lifted = dot(masked[i * B : (i + 1) * B, :], values)
            summed = jnp.sum(rblk[l, i].astype(f32) * lifted, axis=0, keepdims=True)
            for j in range(4):
                rp[l, pl.ds(i * 4 + j, 1), :] = summed[:, j * 128 : (j + 1) * 128]
        away = l != k

        @pl.when(away)
        def _():
            remote(rp.at[l], rq.at[k], q_s.at[l], q_r.at[k], (c, l)).start()

        @pl.when(jnp.logical_not(away))
        def _():
            local(rp.at[l], rq.at[k], q_r.at[k]).start()

        return carry

    lax.fori_loop(0, 8, step, 0)

    for i in range(1, 4):
        ny, nx = (y + i) % 4, (x + i) % 4
        local(wd.at[ny], wd.at[ny], wd_r.at[ny]).wait()
        local(wm.at[nx], wm.at[nx], wm_r.at[nx]).wait()

    def tile_step(t, carry):
        tt[t % 4 // 2, t // 4, t % 2] = dot(wd[t // 4], wm[t % 4])
        return carry

    lax.fori_loop(0, 16, tile_step, 0)
    swap = remote(tt.at[1 - h], trx, tw_s, tw_r, twin)
    swap.start()
    for l in range(8):
        local(rq.at[l], rq.at[l], q_r.at[l]).wait()
    rho[...] = jnp.sum(rq[...], axis=0)

    others(lambda p, to: remote(rho, rg.at[me], g_s, g_r, to).start())
    local(rho, rg.at[me], g_r).start()

    swap.wait_recv()
    side = y // 2

    def to_collect(i):
        target = 2 * h + i
        stays = (target == z) & (side == h)
        return stays, remote(zs.at[i], zr.at[z], zs_s.at[i], zr_r.at[z], (c, target * 2 + side))

    for i in range(2):
        for j in range(4):
            zs[i, j] = (tt[h, j, i] + trx[j, i]).astype(bf16)
        stays, copy = to_collect(i)
        pl.when(jnp.logical_not(stays))(copy.start)

        @pl.when(stays)
        def _():
            local(zs.at[i], zr.at[z], zr_r.at[z]).start()

    lane = lax.broadcasted_iota(jnp.int32, (1, 1, 128), 2) // 32
    low = lax.broadcasted_iota(jnp.int32, (1, 8, 1), 1) < 4
    local(r1, r1, a_r).wait()
    for kk in range(2):
        got = [r1[:, kk * 4 + k4] for k4 in range(4)]
        for p4 in range(4):
            tile = got[p4]
            for k4 in range(4):
                if k4 != p4:
                    turned = pltpu.roll(got[k4], (k4 - p4) % 4 * 32, 2)
                    tile = jnp.where(lane == k4, turned, tile)
            pairs = tile.reshape(8, 2, 8, 128)
            even, odd = pairs[:, 0], pairs[:, 1]
            at_rows, at_cols = pl.ds(p4 * 64, 64), pl.ds(kk * 128, 128)
            xa[at_rows, at_cols] = jnp.where(low, even, pltpu.roll(odd, 4, 1)).reshape(64, 128)
            xa[pl.ds(256 + p4 * 64, 64), at_cols] = jnp.where(low, pltpu.roll(even, 4, 1), odd).reshape(64, 128)

    for copy in loads[2:]:
        copy.wait()
    row_x = x_of_row(lax.broadcasted_iota(jnp.int32, (G, 1), 0))
    sits = row_x == xcell_ref[...]
    local(rg, rg, g_r).wait()
    coef = lax.dot_general(
        tzp[...], rg[...].reshape(8 * ND, QZ), NT,
        precision=lax.Precision.HIGHEST, preferred_element_type=f32,
    )
    sel_first, sel_rows = ROWS["sel_y"]
    sel_y = t1[pl.ds(sel_first, sel_rows), :]
    for i in range(2):
        add = None
        for piece in split2(coef[i : i + 1, :]):
            placed = jnp.where(sits, piece.astype(f32), 0.0).astype(bf16)
            term = dot(placed, sel_y)
            add = term if add is None else add + term
        xa[pl.ds(i * G, G), :] = xa[pl.ds(i * G, G), :] + add

    ty_pair = ty[0:G, :], ty[G : 2 * G, :]
    big[...] = dot3(split2(xa[...]), ty_pair)
    wx = table("wx")
    fields = []
    for i in range(2):
        quad = dot3(wx, split2(big[pl.ds(i * G, G), :]))
        fields.append((quad[:G, :G] - quad[G:, G:], -(quad[G:, :G] + quad[:G, G:])))
    (a_re, a_im), (b_re, b_im) = fields
    xa[0:G, :] = ga[...] * a_re - gb[...] * b_im
    xa[G : 2 * G, :] = ga[...] * a_im + gb[...] * b_re
    back = dot3(split2(xa[...]), ty_pair)
    big[0:G, 0:G] = back[:G, :G] - back[G:, G:]
    big[0:G, G : 2 * G] = back[:G, G:] + back[G:, :G]
    quad = dot3(table("wi"), split2(big[0:G, :]))
    xa[0:G, :] = quad[:G, :G] - quad[G:, G:]
    xa[G : 2 * G, :] = quad[:G, G:] + quad[G:, :G]

    order = lax.broadcasted_iota(jnp.int32, (32, G), 0)
    block = order % 16 * 2 + order // 16
    row_of = x_of_row(lax.broadcasted_iota(jnp.int32, (32, G), 1))
    pick = (row_of == own_ref[...] * 16 + block % 16).astype(f32).astype(bf16)
    line = lax.broadcasted_iota(jnp.int32, (32, G), 1)
    valid = line % 32 // 4 == block // 16
    rows = []
    for i in range(2):
        hi, lo = split2(xa[pl.ds(i * G, G), :])
        here = jnp.where(valid, dot(pick, hi) + dot(pick, lo), 0.0)
        rows += [here[0:16], here[16:32]]
    hi, lo = split2(jnp.concatenate(rows, axis=1))
    packed = dot(hi, selc[...]) + dot(lo, selc[...])
    for i in range(16):
        s3[i] = packed[i : i + 1, :]
    others(lambda p, to: remote(s3.at[p // 8], r3.at[me], p_s, p_r, to).start())
    local(s3.at[c], r3.at[me], p_r).start()

    collects = h == side

    def to_owner(j):
        ny = (y + j) % 4
        return remote(ys.at[ny], yr.at[y % 2], ys_s.at[j - 1], yr_r.at[y % 2], (x * 4 + ny, k))

    @pl.when(collects)
    def _():
        for i in range(4):
            local(zr.at[i], zr.at[i], zr_r.at[i]).wait()
        for j in range(4):
            total = zr[0, j].astype(f32) + zr[1, j].astype(f32) + (zr[2, j].astype(f32) + zr[3, j].astype(f32))
            ys[j] = total.astype(bf16)
        for j in range(1, 4):
            to_owner(j).start()
        local(ys.at[y], yr.at[y % 2], yr_r.at[y % 2]).start()

    for kk in range(2):
        tiles = []
        at_cols = pl.ds(kk * 128, 128)
        for p4 in range(4):
            re = xa[pl.ds(p4 * 64, 64), at_cols].reshape(8, 8, 128)
            im = xa[pl.ds(256 + p4 * 64, 64), at_cols].reshape(8, 8, 128)
            even = jnp.where(low, re, pltpu.roll(im, 4, 1))
            odd = jnp.where(low, pltpu.roll(re, 4, 1), im)
            tiles.append(jnp.stack([even, odd], axis=1).reshape(16, 8, 128))
        for k4 in range(4):
            tile = tiles[k4]
            for p4 in range(4):
                if p4 != k4:
                    tile = jnp.where(lane == p4, pltpu.roll(tiles[p4], (p4 - k4) % 4 * 32, 2), tile)
            s2[:, kk * 4 + k4] = tile
    others(lambda p, to: remote(s2.at[p // 8, p % 8], r2.at[me], b_s, b_r, to).start())
    local(s2.at[c, k], r2.at[me], b_r).start()

    local(r3, r3, p_r).wait()
    arrived = split2(r3[...].reshape(ND, 128))
    both = dot3(arrived, table("tp"), TN)
    rho_pot = both[:64, :128] + both[64:, 128:]
    for i in range(2):
        for l in range(8):
            for j in range(4):
                at_row = i * 32 + l * 4 + j
                scaled = rblk[l, i, :, pl.ds(j * 128, 128)].astype(f32) * rho_pot[at_row : at_row + 1, :]
                wt[pl.ds(i * B, B), pl.ds(l * CH + j * 128, 128)] = scaled.astype(bf16)
    for j in range(4):
        for i in range(2):
            block_sum = dot(wt[pl.ds(i * B, B), :], phi[j], NT)
            har_ref[pl.ds(i * B, B), pl.ds(j * B, B)] = (block_sum * pat_ref[i, j].astype(f32)).astype(bf16)

    local(r2, r2, b_r).wait()
    tzi = table("tzi")
    for j in range(4):
        got = jnp.concatenate([r2[:, j, :], r2[:, 4 + j, :]], axis=0)
        pot_ref[pl.ds(j * 128, 128), :] = dot3(split2(got), tzi, TN)

    for i in range(2):
        local(yr.at[i], yr.at[i], yr_r.at[i]).wait()
        prod_ref[:, pl.ds(i * B, B)] = yr[i] * keep_ref[0, i].astype(f32).astype(bf16)

    for copy in rows_out + cols_out + [swap]:
        copy.wait_send()
    for i in range(2):
        stays, copy = to_collect(i)
        pl.when(jnp.logical_not(stays))(copy.wait_send)

    @pl.when(collects)
    def _():
        for j in range(1, 4):
            to_owner(j).wait_send()

    for when, copy in to_send:
        pl.when(when)(copy.wait_send)
    for dx in range(1, 4):
        l = 2 * ((x + dx) % 4) + h

        @pl.when(far)
        def _():
            remote(rblk.at[l], rblk.at[l], ssem.at[fwd + dx], rsem.at[l], twin).wait_send()

    for l in range(8):

        @pl.when(l != k)
        def _():
            remote(rp.at[l], rq.at[k], q_s.at[l], q_r.at[k], (c, l)).wait_send()

    most = pl.ds(0, ND - 1)
    for src, sem in ((s1, a_s), (rg, g_s), (r3, p_s), (r2, b_s)):
        local(src.at[most], src.at[most], sem).wait()


def main_call(density, pattern, margin, ovl, keep, basis, rest, slab_owner, lengths):
    t1, ty, selc, tzp = tables()
    blocks = jnp.arange(32, dtype=jnp.int32)
    x_cells = slab_owner * 16 + blocks % 16
    xcell = jnp.broadcast_to(x_cells.reshape(16, 1, 2, 1), (16, 8, 2, 4)).reshape(1, 1024)
    order = slab_owner.reshape(16, 2).T.reshape(32, 1)
    vmem = pl.BlockSpec(memory_space=pltpu.VMEM)
    smem = pl.BlockSpec(memory_space=pltpu.SMEM)
    hbm = pl.BlockSpec(memory_space=pl.ANY)
    V = pltpu.VMEM
    D = pltpu.SemaphoreType.DMA
    return pl.pallas_call(
        kernel,
        out_shape=(
            jax.ShapeDtypeStruct((512, G), f32),
            jax.ShapeDtypeStruct((512, 1024), bf16),
            jax.ShapeDtypeStruct((B, 2 * B), bf16),
        ),
        in_specs=[smem] * 4 + [vmem, vmem, hbm, vmem, vmem, vmem, hbm, hbm, hbm, hbm],
        out_specs=(vmem, vmem, vmem),
        scratch_shapes=[
            V((4, B, 4096), bf16),
            V((8, 2, B, CH), bf16),
            V((3, 2, B, CH), bf16),
            V((512, 1024), bf16),
            V((512, 4096), bf16),
            V((T1_ROWS, G), bf16),
            V((2 * G, 2 * G), bf16),
            V((1024, 128), bf16),
            V((8, 128), f32),
            V((ND, 8, 128), f32),
            V((16, 8, 8, 128), f32),
            V((16, 8, 8, 128), f32),
            V((ND, 8, 128), f32),
            V((16, 1, 128), f32),
            V((ND, 1, 128), f32),
            V((8, 8, 128), f32),
            V((8, 8, 128), f32),
            V((8, 128), f32),
            V((ND, 8, 128), f32),
            V((2 * G, G), f32),
            V((G, G), f32),
            V((G, G), f32),
            V((2 * G, 2 * G), f32),
            V((4, B, 1024), bf16),
            V((4, 1024, B), bf16),
            V((2, 4, 2, B, B), f32),
            V((4, 2, B, B), f32),
            V((2, 4, B, B), bf16),
            V((4, 4, B, B), bf16),
            V((4, B, B), bf16),
            V((2, B, B), bf16),
            D((5,)),
            D((3,)),
            D((8,)),
            D((32,)),
            D(()),
            D(()),
            D((8,)),
            D((8,)),
            D(()),
            D(()),
            D(()),
            D(()),
            D(()),
            D(()),
            D((3,)),
            D((4,)),
            D((3,)),
            D((4,)),
            D(()),
            D(()),
            D((2,)),
            D((4,)),
            D((3,)),
            D((2,)),
        ],
        compiler_params=pltpu.CompilerParams(
            collective_id=0, has_side_effects=True, vmem_limit_bytes=58 << 20
        ),
        cost_estimate=pl.CostEstimate(flops=12 * 10**9, bytes_accessed=24 << 20, transcendentals=0),
    )(pattern, lengths, ovl, keep, margin, density, basis, rest, xcell, order, t1, ty, selc, tzp)


def per_device(
    density, dens_pattern, margin_window, ovl_pattern, keep_mask, basis_values, rest_density,
    slab_owner, cell_lengths,
):
    potential, hartree, product = main_call(
        density, dens_pattern, margin_window, ovl_pattern, keep_mask, basis_values,
        rest_density.reshape(512, G), slab_owner, cell_lengths,
    )
    return potential.reshape(16, 32, G), hartree, product


def solution(mesh):
    return jax.shard_map(
        per_device,
        mesh=mesh,
        in_specs=(
            P("clus", "col"),
            P("clus", "col"),
            P("col", "clus"),
            P("col", "clus"),
            P("clus", "col"),
            P("col", None, None),
            P("clus", "col", None),
            P(),
            P(),
        ),
        out_specs=(P("clus", "col", None), P("clus", "col"), P("clus", "col")),
        check_vma=False,
    )
```

```python
import functools
import math

import jax
import jax.numpy as jnp
import ml_dtypes
import numpy as np
from jax import lax
from jax.experimental import pallas as pl
from jax.experimental.pallas import tpu as pltpu
from jax.sharding import PartitionSpec as P

B = 256
G = 256
QZ = 128
NX, NY, NZ = 4, 4, 4
ND = 128
CH = 128
NCH = 32
SHARE = (5, 5, 1, 5)
FIRST = (0, 5, 10, 11)
MOST = 5
four_pi = 4.0 * math.pi
f32 = jnp.float32
bf16 = jnp.bfloat16
MESH = pl.DeviceIdType.MESH
NT = (((1,), (1,)), ((), ()))
TN = (((0,), (0,)), ((), ()))
NN = (((1,), (0,)), ((), ()))


def split_np(a):
    hi = a.astype(np.float32).astype(ml_dtypes.bfloat16)
    lo = (a - hi.astype(np.float64)).astype(np.float32).astype(ml_dtypes.bfloat16)
    return [hi, lo]


def x_of_row(row):
    return (row % 64) // 4 * 16 + row % 4 * 4 + row // 64


@functools.lru_cache(maxsize=1)
def tables():
    n = np.arange(G)
    ang = 2.0 * np.pi * (n[:, None] * n[None, :] % G) / G
    cos, sin = np.cos(ang), np.sin(ang)
    half = cos[:128], sin[:128]
    tz = np.concatenate([half[0], -half[1]], 0)
    tz[128] = cos[128]
    tzi = np.concatenate([2.0 * half[0], -2.0 * half[1]], 0)
    tzi[0] = 1.0
    tzi[128] = cos[128]
    tzi = tzi / float(G) ** 3
    perm = x_of_row(n)
    wx = np.concatenate([cos[:, perm], sin[:, perm]], 0)
    wi = np.concatenate([cos[perm], sin[perm]], 0)
    tq = np.concatenate([tz[:128, 64:192], tz[128:, 64:192]], 1)
    kc = np.arange(ND) % 16 * 8 + np.arange(ND) // 16
    tzi = np.concatenate([tzi[:128][kc], tzi[128:][kc]], 0)
    tp = np.concatenate([tzi[:128, 64:192], tzi[128:, 64:192]], 1)
    t1 = np.concatenate(sum([split_np(a) for a in (tz, tzi, wx, wi, tp, tq)], []), 0)
    ty = np.concatenate(split_np(np.concatenate([cos, sin], 1)), 0)
    row = np.arange(1024)
    ri, il, y = row // 512, row // 256 % 2, row % 256
    lane = ri * 64 + il * 32 + y // 32 * 4 + y % 4
    sel_c = (lane[:, None] == np.arange(128)[None, :]) & (y % 32 < 8)[:, None]
    sel_c = sel_c.astype(np.float32).astype(ml_dtypes.bfloat16)
    return t1, ty, sel_c


ROWS = {}
at = 0
for name, rows in (
    ("tz", 256), ("tzi", 256), ("wx", 512), ("wi", 512), ("tp", 128), ("tq", 128)
):
    ROWS[name] = (at, rows)
    at += 2 * rows
T1_ROWS = at


def split2(a):
    hi = a.astype(bf16)
    lo = (a - hi.astype(f32)).astype(bf16)
    return hi, lo


def dot(a, b, dims=NN):
    return lax.dot_general(a, b, dims, preferred_element_type=f32)


def dot3(a, b, dims=NN):
    return dot(a[0], b[0], dims) + (dot(a[0], b[1], dims) + dot(a[1], b[0], dims))


def kernel(
    pat_ref, len_ref, ovl_ref, keep_ref, margin_ref, own_ref, dens_ref, phi_ref, rest_ref,
    t1_hbm, ty_hbm, selc_hbm,
    pot_out, har_out, prod_out,
    pot_ref, har_ref, prod_ref,
    phi, rblk, relay, masked, wt, t1, ty, selc,
    s1, x1, r1, s2, x2, r2, s3, x3, r3, v1, xv, rv, rp, rq, pad, xa, ga, gb, big,
    wd, wm, tt, trx, zs, zr, ys, yr,
    lsem, tsem, rsem, ssem, fsem, q_s, q_r,
    a1_s, a1_r, a2_s, a2_r, g1_s, g1_r, g2_s, g2_r, p1_s, p1_r, p2_s, p2_r, b1_s, b1_r, b2_s, b2_r,
    wd_s, wd_r, wm_s, wm_r, tw_s, tw_r, zs_s, zr_r, ys_s, yr_r, osem,
):
    c = lax.axis_index("clus")
    k = lax.axis_index("col")
    me = c * 8 + k
    x, y = c // 4, c % 4
    z, h = k // 2, k % 2
    zp, zm, z2 = (z + 1) % 4, (z + 3) % 4, (z + 2) % 4
    root = h == y // 2
    hub = x == z
    far = jnp.logical_not(hub)
    twin = (c, z * 2 + 1 - h)

    def part(name, lo):
        first, rows = ROWS[name]
        return t1[pl.ds(first + lo * rows, rows), :]

    def table(name):
        return part(name, 0), part(name, 1)

    def local(src, dst, sem):
        return pltpu.make_async_copy(src, dst, sem)

    def remote(src, dst, send, recv, to):
        return pltpu.make_async_remote_copy(
            src_ref=src, dst_ref=dst, send_sem=send, recv_sem=recv, device_id=to, device_id_type=MESH
        )

    def clus_group(src_of, dst, send_sem, recv_sem):
        def body(i, carry):
            to = lax.rem(c + i, 16)
            remote(src_of(to), dst.at[c], send_sem, recv_sem, (to, k)).start()
            return carry

        lax.fori_loop(1, 16, body, 0)
        local(src_of(c), dst.at[c], recv_sem).start()

    def col_group(src_of, dst, send_sem, recv_sem):
        for i in range(1, 8):
            to = (k + i) % 8
            remote(src_of(to), dst.at[k], send_sem, recv_sem, (c, to)).start()
        local(src_of(k), dst.at[k], recv_sem).start()

    bar = pltpu.get_barrier_semaphore()

    def greet(i, carry):
        pl.semaphore_signal(bar, inc=1, device_id=(lax.rem(c + i, 16), k), device_id_type=MESH)
        return carry

    lax.fori_loop(1, 16, greet, 0)
    for i in range(1, 8):
        pl.semaphore_signal(bar, inc=1, device_id=(c, (k + i) % 8), device_id_type=MESH)
    loads = [
        local(t1_hbm, t1, lsem.at[0]),
        local(phi_ref, phi, lsem.at[1]),
        local(ty_hbm, ty, lsem.at[2]),
        local(selc_hbm, selc, lsem.at[3]),
    ]
    for copy in loads:
        copy.start()
    for i in range(2):
        for j in range(4):
            keep = pat_ref[i, j].astype(f32).astype(bf16)
            at_rows, at_cols = pl.ds(i * B, B), pl.ds(j * B, B)
            masked[at_rows, at_cols] = dens_ref[at_rows, at_cols] * keep
    wd[y] = masked[0:B, :]
    for j in range(4):
        at_rows = pl.ds(j * B, B)
        wm[x, at_rows, :] = margin_ref[at_rows, :] * ovl_ref[0, j].astype(f32).astype(bf16)
    loads[0].wait()
    lines = dot3(table("tz"), split2(rest_ref[...].reshape(512, G)), NT)
    for i in range(2):
        for j in range(4):
            s1[:, i * 4 + j, :] = lines[i * 128 : (i + 1) * 128, j * 128 : (j + 1) * 128]
    loads[1].wait()
    pl.semaphore_wait(bar, 22)

    to_y = [(x * 4 + (y + i) % 4, k) for i in range(1, 4)]
    to_x = [((x + i) % 4 * 4 + y, k) for i in range(1, 4)]
    rows_out = [remote(wd.at[y], wd.at[y], wd_s.at[i], wd_r.at[y], to) for i, to in enumerate(to_y)]
    cols_out = [remote(wm.at[x], wm.at[x], wm_s.at[i], wm_r.at[x], to) for i, to in enumerate(to_x)]
    for copy in rows_out:
        copy.start()

    first = 2 * (y % 2)

    def own_part(g):
        return phi.at[pl.ds(first, 2), :, pl.ds(pl.multiple_of(g * CH, CH), CH)]

    to_send = []

    def send(when, src, dst, recv, to):
        index = len(to_send)
        copy = remote(src, dst, ssem.at[index], recv, to)
        to_send.append((when, copy))
        pl.when(when)(copy.start)

    def share(dist):
        pair, count = FIRST[0], SHARE[0]
        for d in range(1, 4):
            pair = jnp.where(dist == d, FIRST[d], pair)
            count = jnp.where(dist == d, SHARE[d], count)
        return pair, count

    my_pair, my_count = share((x - z) % 4)

    def batch(i):
        for turn in range(2):
            for up in (True, False):
                half = turn if up else 1 - turn
                slot = 0 if up else 1
                send(
                    root & (i < my_count), own_part(jnp.minimum(2 * (my_pair + i) + half, NCH - 1)),
                    relay.at[slot, i], tsem.at[slot, i], (c, (zp if up else zm) * 2 + half),
                )

    batch(0)
    batch(1)

    clus_group(lambda to: s1.at[pl.ds(pl.multiple_of(to * 8, 8), 8)], x1, a1_s, a1_r)
    for copy in cols_out:
        copy.start()

    hub_root = hub & root

    @pl.when(hub_root)
    def _():
        def body(g, carry):
            remote(own_part(g), rblk.at[g], fsem.at[g], rsem.at[g], twin).start()
            local(own_part(g), rblk.at[g], rsem.at[g]).start()
            return carry

        lax.fori_loop(0, NCH, body, 0)

    row_id = lax.broadcasted_iota(jnp.int32, (G, G), 0)
    col_id = lax.broadcasted_iota(jnp.int32, (G, G), 1)

    def wave(freq, axis):
        signed = jnp.where(freq < G // 2, freq, freq - G).astype(f32)
        scaled = signed * (2.0 * math.pi) / jnp.full(freq.shape, len_ref[axis], f32)
        return scaled * scaled

    flat = wave(row_id, 0) + wave(col_id, 1)
    for out, kz in ((ga, me), (gb, jnp.where(me == 0, 128, me))):
        kz = jnp.full((G, G), kz, jnp.int32)
        anchor = (row_id == 0) & (col_id == 0) & (kz == 0)
        out[...] = jnp.where(anchor, 0.0, four_pi / jnp.where(anchor, 1.0, flat + wave(kz, 2)))

    stages = []
    for i in range(MOST + 1):
        if i < MOST:
            stages += [(0, i), (1, i)]
        if i:
            stages.append((2, i - 1))
    for slot, i in stages:
        plane = (zm, zp, z2)[slot]
        pair, count = share((x - plane) % 4)
        have = i < count

        @pl.when(have)
        def _():
            local(relay.at[slot, i], relay.at[slot, i], tsem.at[slot, i]).wait()

        if slot == 1 and i + 2 < MOST:
            batch(i + 2)
        if slot == 0:
            send(have & (h == 0), relay.at[0, i], relay.at[2, i], tsem.at[2, i], (c, zp * 2))
        if slot == 1:
            send(have & (h == 1), relay.at[1, i], relay.at[2, i], tsem.at[2, i], (c, zm * 2 + 1))
        here = plane == x
        g = jnp.minimum(2 * (pair + i) + h, NCH - 1)
        send(have & here, relay.at[slot, i], rblk.at[g], rsem.at[g], twin)
        send(have & jnp.logical_not(here), relay.at[slot, i], rblk.at[g], rsem.at[g], (plane * 4 + y, k))

        @pl.when(have & here)
        def _():
            local(relay.at[slot, i], rblk.at[g], rsem.at[g]).start()

    local(x1, x1, a1_r).wait()
    col_group(lambda to: x1.at[:, to], r1, a2_s, a2_r)

    def pair_at(t):
        i, line = t // 3, t % 3
        return jnp.where(t == 15, 10, jnp.where(line == 0, i, jnp.where(line == 1, 5 + i, 11 + i)))

    def passed_on(pair):
        g = 2 * pair + h
        return far & (pair >= 5), remote(rblk.at[g], rblk.at[g], fsem.at[g], rsem.at[g], twin)

    def step(t, carry):
        @pl.when(t < 16)
        def _():
            pair = pair_at(t)
            g = 2 * pair + h
            local(rblk.at[g], rblk.at[g], rsem.at[g]).wait()
            when, copy = passed_on(pair)
            pl.when(when)(copy.start)

        @pl.when(t > 0)
        def _():
            pair = pair_at(t - 1)
            g = 2 * pair + 1 - h
            local(rblk.at[g], rblk.at[g], rsem.at[g]).wait()
            cells = pl.ds(pl.multiple_of(pair * 2 * CH, 2 * CH), 2 * CH)
            values = phi[:, :, cells].reshape(4 * B, 2 * CH)
            for i in range(2):
                lifted = dot(masked[i * B : (i + 1) * B, :], values)
                for j in range(2):
                    basis = rblk[2 * pair + j, i].astype(f32)
                    summed = jnp.sum(basis * lifted[:, j * CH : (j + 1) * CH], axis=0, keepdims=True)
                    rp[pair // 2, pl.ds(i * 4 + pair % 2 * 2 + j, 1), :] = summed

        return carry

    lax.fori_loop(0, 17, step, 0)
    for l in range(8):
        away = l != k

        @pl.when(away)
        def _():
            remote(rp.at[l], rq.at[k], q_s.at[l], q_r.at[k], (c, l)).start()

        @pl.when(jnp.logical_not(away))
        def _():
            local(rp.at[l], rq.at[k], q_r.at[k]).start()

    for i in range(1, 4):
        ny, nx = (y + i) % 4, (x + i) % 4
        local(wd.at[ny], wd.at[ny], wd_r.at[ny]).wait()
        local(wm.at[nx], wm.at[nx], wm_r.at[nx]).wait()

    def tile_step(t, carry):
        tt[t % 4 // 2, t // 4, t % 2] = dot(wd[t // 4], wm[t % 4])
        return carry

    lax.fori_loop(0, 16, tile_step, 0)
    swap = remote(tt.at[1 - h], trx, tw_s, tw_r, twin)
    swap.start()
    for l in range(8):
        local(rq.at[l], rq.at[l], q_r.at[l]).wait()
    rho = jnp.sum(rq[...], axis=0)

    pad[...] = jnp.zeros_like(pad)
    pad[0:8, 0:128] = rho
    pad[8:16, 128:256] = rho
    for copy in loads[2:]:
        copy.wait()
    v1[...] = dot3(table("tq"), split2(pad[...]), NT).reshape(ND, 1, 128)
    clus_group(lambda to: v1.at[pl.ds(to * 8, 8)], xv, g1_s, g1_r)

    local(xv, xv, g1_r).wait()
    col_group(lambda to: xv.at[:, to], rv, g2_s, g2_r)

    lane = lax.broadcasted_iota(jnp.int32, (1, 1, 128), 2) // 32
    low = lax.broadcasted_iota(jnp.int32, (1, 8, 1), 1) < 4
    local(r1, r1, a2_r).wait()
    for kk in range(2):
        got = [r1[kk * 4 + k4] for k4 in range(4)]
        for p4 in range(4):
            tile = got[p4]
            for k4 in range(4):
                if k4 != p4:
                    turned = pltpu.roll(got[k4], (k4 - p4) % 4 * 32, 2)
                    tile = jnp.where(lane == k4, turned, tile)
            pairs = tile.reshape(8, 2, 8, 128)
            even, odd = pairs[:, 0], pairs[:, 1]
            at_rows, at_cols = pl.ds(p4 * 64, 64), pl.ds(kk * 128, 128)
            xa[at_rows, at_cols] = jnp.where(low, even, pltpu.roll(odd, 4, 1)).reshape(64, 128)
            xa[pl.ds(256 + p4 * 64, 64), at_cols] = jnp.where(low, pltpu.roll(even, 4, 1), odd).reshape(64, 128)

    def block_of(row):
        return row % 16 * 2 + row // 16

    spot = lax.broadcasted_iota(jnp.int32, (1, 32), 1)
    x_cell = jnp.zeros((1, 32), jnp.int32)
    order = lax.broadcasted_iota(jnp.int32, (32, G), 0)
    x_pick = jnp.zeros((32, G), jnp.int32)
    for row in range(32):
        cell = own_ref[block_of(row)] * 16 + block_of(row) % 16
        x_cell = jnp.where(spot == row, cell, x_cell)
        x_pick = jnp.where(order == row, cell, x_pick)
    row_x = x_of_row(lax.broadcasted_iota(jnp.int32, (G, 1), 0))
    sits = (row_x == x_cell).astype(f32).astype(bf16)
    lane_id = lax.broadcasted_iota(jnp.int32, (16, 128), 1)
    upper = lax.broadcasted_iota(jnp.int32, (16, 128), 0) // 8
    valid_lane = lane_id % 32 // 4 == upper
    swap.wait_recv()
    side = y // 2

    def to_collect(i):
        target = 2 * h + i
        stays = (target == z) & (side == h)
        return stays, remote(zs.at[i], zr.at[z], zs_s.at[i], zr_r.at[z], (c, target * 2 + side))

    for i in range(2):
        for j in range(4):
            zs[i, j] = (tt[h, j, i] + trx[j, i]).astype(bf16)
        stays, copy = to_collect(i)
        pl.when(jnp.logical_not(stays))(copy.start)

        @pl.when(stays)
        def _():
            local(zs.at[i], zr.at[z], zr_r.at[z]).start()

    local(rv, rv, g2_r).wait()
    spread = []
    for half in range(2):
        acc = None
        for l4 in range(4):
            values = rv[half * 4 + l4].reshape(16, 128)
            if l4:
                values = pltpu.roll(values, l4 * 32, 1)
            acc = values if acc is None else jnp.where(lane_id // 32 == l4, values, acc)
        spread.append(acc)
    for i in range(2):
        rows = []
        for il in range(2):
            offset = i * 8 + il * 4
            halves = []
            for acc in spread:
                low_row = pltpu.roll(acc, (128 - offset) % 128, 1) if offset else acc
                high_row = pltpu.roll(acc, (132 - offset) % 128, 1) if offset != 4 else acc
                halves.append(jnp.where(valid_lane, jnp.where(upper == 0, low_row, high_row), 0.0))
            rows.append(jnp.concatenate(halves, axis=1))
        hi, lo = split2(jnp.concatenate(rows, axis=0))
        xa[pl.ds(i * G, G), :] = xa[pl.ds(i * G, G), :] + (dot(sits, hi) + dot(sits, lo))

    ty_pair = ty[0:G, :], ty[G : 2 * G, :]
    big[...] = dot3(split2(xa[...]), ty_pair)
    wx = table("wx")
    fields = []
    for i in range(2):
        quad = dot3(wx, split2(big[pl.ds(i * G, G), :]))
        fields.append((quad[:G, :G] - quad[G:, G:], -(quad[G:, :G] + quad[:G, G:])))
    (a_re, a_im), (b_re, b_im) = fields
    xa[0:G, :] = ga[...] * a_re - gb[...] * b_im
    xa[G : 2 * G, :] = ga[...] * a_im + gb[...] * b_re
    back = dot3(split2(xa[...]), ty_pair)
    big[0:G, 0:G] = back[:G, :G] - back[G:, G:]
    big[0:G, G : 2 * G] = back[:G, G:] + back[G:, :G]
    quad = dot3(table("wi"), split2(big[0:G, :]))
    xa[0:G, :] = quad[:G, :G] - quad[G:, G:]
    xa[G : 2 * G, :] = quad[:G, G:] + quad[G:, :G]

    row_of = x_of_row(lax.broadcasted_iota(jnp.int32, (32, G), 1))
    pick = (row_of == x_pick).astype(f32).astype(bf16)
    line = lax.broadcasted_iota(jnp.int32, (32, G), 1)
    valid = line % 32 // 4 == order % 16 // 8
    rows = []
    for i in range(2):
        hi, lo = split2(xa[pl.ds(i * G, G), :])
        here = jnp.where(valid, dot(pick, hi) + dot(pick, lo), 0.0)
        rows += [here[0:16], here[16:32]]
    hi, lo = split2(jnp.concatenate(rows, axis=1))
    packed = dot(hi, selc[...]) + dot(lo, selc[...])
    for i in range(16):
        s3[i] = packed[i : i + 1, :]
    clus_group(lambda to: s3.at[to], x3, p1_s, p1_r)

    for kk in range(2):
        tiles = []
        at_cols = pl.ds(kk * 128, 128)
        for p4 in range(4):
            re = xa[pl.ds(p4 * 64, 64), at_cols].reshape(8, 8, 128)
            im = xa[pl.ds(256 + p4 * 64, 64), at_cols].reshape(8, 8, 128)
            even = jnp.where(low, re, pltpu.roll(im, 4, 1))
            odd = jnp.where(low, pltpu.roll(re, 4, 1), im)
            tiles.append(jnp.stack([even, odd], axis=1).reshape(16, 8, 128))
        for k4 in range(4):
            tile = tiles[k4]
            for p4 in range(4):
                if p4 != k4:
                    tile = jnp.where(lane == p4, pltpu.roll(tiles[p4], (p4 - k4) % 4 * 32, 2), tile)
            s2[:, kk * 4 + k4] = tile
    clus_group(lambda to: s2.at[to], x2, b1_s, b1_r)
    local(x3, x3, p1_r).wait()
    col_group(lambda to: x3, r3, p2_s, p2_r)

    collects = h == side

    def to_owner(j):
        ny = (y + j) % 4
        return remote(ys.at[ny], yr.at[y % 2], ys_s.at[j - 1], yr_r.at[y % 2], (x * 4 + ny, k))

    @pl.when(collects)
    def _():
        for i in range(4):
            local(zr.at[i], zr.at[i], zr_r.at[i]).wait()
        for j in range(4):
            total = zr[0, j].astype(f32) + zr[1, j].astype(f32) + (zr[2, j].astype(f32) + zr[3, j].astype(f32))
            ys[j] = total.astype(bf16)
        for j in range(1, 4):
            to_owner(j).start()
        local(ys.at[y], yr.at[y % 2], yr_r.at[y % 2]).start()

    local(r3, r3, p2_r).wait()
    arrived = split2(r3[...].reshape(ND, 128))
    both = dot3(arrived, table("tp"), TN)
    rho_pot = both[:64, :128] + both[64:, 128:]
    for i in range(2):
        for g in range(NCH):
            at_row = i * 32 + g
            scaled = rblk[g, i].astype(f32) * rho_pot[at_row : at_row + 1, :]
            wt[pl.ds(i * B, B), pl.ds(g * CH, CH)] = scaled.astype(bf16)
    for j in range(4):
        if j == 2:
            local(x2, x2, b1_r).wait()
            col_group(lambda to: x2.at[:, to], r2, b2_s, b2_r)
        for i in range(2):
            block_sum = dot(wt[pl.ds(i * B, B), :], phi[j], NT)
            har_ref[pl.ds(i * B, B), pl.ds(j * B, B)] = (block_sum * pat_ref[i, j].astype(f32)).astype(bf16)

    done = [local(har_ref, har_out, osem.at[0])]
    done[0].start()
    local(r2, r2, b2_r).wait()
    lines_back = r2[...].reshape(ND, 8, 128)
    tzi = table("tzi")
    for j in range(4):
        got = jnp.concatenate([lines_back[:, j, :], lines_back[:, 4 + j, :]], axis=0)
        pot_ref[pl.ds(j * 4, 4)] = dot3(split2(got), tzi, TN).reshape(4, 32, G)

    done.append(local(pot_ref, pot_out, osem.at[1]))
    done[1].start()
    for i in range(2):
        local(yr.at[i], yr.at[i], yr_r.at[i]).wait()
        prod_ref[:, pl.ds(i * B, B)] = yr[i] * keep_ref[0, i].astype(f32).astype(bf16)

    done.append(local(prod_ref, prod_out, osem.at[2]))
    done[2].start()

    for copy in rows_out + cols_out + [swap]:
        copy.wait_send()
    for i in range(2):
        stays, copy = to_collect(i)
        pl.when(jnp.logical_not(stays))(copy.wait_send)

    @pl.when(collects)
    def _():
        for j in range(1, 4):
            to_owner(j).wait_send()

    for when, copy in to_send:
        pl.when(when)(copy.wait_send)

    def leave(g, carry):
        remote(rblk.at[g], rblk.at[g], fsem.at[g], rsem.at[g], twin).wait_send()
        return carry

    @pl.when(hub_root)
    def _():
        lax.fori_loop(0, NCH, leave, 0)

    @pl.when(far)
    def _():
        lax.fori_loop(5, 16, lambda pair, carry: leave(2 * pair + h, carry), 0)

    for l in range(8):

        @pl.when(l != k)
        def _():
            remote(rp.at[l], rq.at[k], q_s.at[l], q_r.at[k], (c, l)).wait_send()

    for dst, sem in ((x1, a1_s), (xv, g1_s), (x3, p1_s), (x2, b1_s)):
        rest_of = dst.at[pl.ds(0, 15)]
        local(rest_of, rest_of, sem).wait()
    for dst, sem in ((r1, a2_s), (rv, g2_s), (r3, p2_s), (r2, b2_s)):
        rest_of = dst.at[pl.ds(0, 7)]
        local(rest_of, rest_of, sem).wait()
    for copy in done:
        copy.wait()


def hand_over(*refs):
    arrays, outs, held, sem = refs[:3], refs[3:6], refs[6:9], refs[9]
    into = [pltpu.make_async_copy(arrays[i], held[i], sem.at[i]) for i in range(3)]
    away = [pltpu.make_async_copy(held[i], outs[i], sem.at[3 + i]) for i in range(3)]
    for copy in into:
        copy.start()
    for i in (2, 0, 1):
        into[i].wait()
        away[i].start()
    for copy in away:
        copy.wait()


def final_copy(arrays):
    hbm = pl.BlockSpec(memory_space=pl.ANY)
    return pl.pallas_call(
        hand_over,
        out_shape=tuple(jax.ShapeDtypeStruct(a.shape, a.dtype) for a in arrays),
        in_specs=[hbm] * 3,
        out_specs=(hbm,) * 3,
        scratch_shapes=[pltpu.VMEM(a.shape, a.dtype) for a in arrays] + [pltpu.SemaphoreType.DMA((6,))],
        compiler_params=pltpu.CompilerParams(vmem_limit_bytes=62 << 20),
        cost_estimate=pl.CostEstimate(flops=0, bytes_accessed=4 << 20, transcendentals=0),
    )(*arrays)


def main_call(density, pattern, margin, ovl, keep, basis, rest, slab_owner, lengths):
    t1, ty, selc = tables()
    vmem = pl.BlockSpec(memory_space=pltpu.VMEM)
    smem = pl.BlockSpec(memory_space=pltpu.SMEM)
    hbm = pl.BlockSpec(memory_space=pl.ANY)
    V = pltpu.VMEM
    D = pltpu.SemaphoreType.DMA
    return pl.pallas_call(
        kernel,
        out_shape=(
            jax.ShapeDtypeStruct((16, 32, G), f32),
            jax.ShapeDtypeStruct((512, 1024), bf16),
            jax.ShapeDtypeStruct((B, 2 * B), bf16),
        ),
        in_specs=[smem] * 4 + [vmem, smem, vmem, hbm, vmem, hbm, hbm, hbm],
        out_specs=(hbm, hbm, hbm),
        scratch_shapes=[
            V((16, 32, G), f32),
            V((512, 1024), bf16),
            V((B, 2 * B), bf16),
            V((4, B, 4096), bf16),
            V((NCH, 2, B, CH), bf16),
            V((3, MOST, 2, B, CH), bf16),
            V((512, 1024), bf16),
            V((512, 4096), bf16),
            V((T1_ROWS, G), bf16),
            V((2 * G, 2 * G), bf16),
            V((1024, 128), bf16),
            V((ND, 8, 128), f32),
            V((16, 8, 8, 128), f32),
            V((8, 16, 8, 128), f32),
            V((16, 8, 8, 128), f32),
            V((16, 8, 8, 128), f32),
            V((8, 16, 8, 128), f32),
            V((16, 1, 128), f32),
            V((16, 1, 128), f32),
            V((8, 16, 1, 128), f32),
            V((ND, 1, 128), f32),
            V((16, 8, 1, 128), f32),
            V((8, 16, 1, 128), f32),
            V((8, 8, 128), f32),
            V((8, 8, 128), f32),
            V((128, 2 * 128), f32),
            V((2 * G, G), f32),
            V((G, G), f32),
            V((G, G), f32),
            V((2 * G, 2 * G), f32),
            V((4, B, 1024), bf16),
            V((4, 1024, B), bf16),
            V((2, 4, 2, B, B), f32),
            V((4, 2, B, B), f32),
            V((2, 4, B, B), bf16),
            V((4, 4, B, B), bf16),
            V((4, B, B), bf16),
            V((2, B, B), bf16),
            D((5,)),
            D((3, MOST)),
            D((NCH,)),
            D((64,)),
            D((NCH,)),
            D((8,)),
            D((8,)),
            *([D(())] * 16),
            D((3,)),
            D((4,)),
            D((3,)),
            D((4,)),
            D(()),
            D(()),
            D((2,)),
            D((4,)),
            D((3,)),
            D((2,)),
            D((3,)),
        ],
        compiler_params=pltpu.CompilerParams(
            collective_id=0, has_side_effects=True, vmem_limit_bytes=58 << 20
        ),
        cost_estimate=pl.CostEstimate(flops=12 * 10**9, bytes_accessed=24 << 20, transcendentals=0),
    )(pattern, lengths, ovl, keep, margin, slab_owner, density, basis, rest, t1, ty, selc)


def per_device(
    density, dens_pattern, margin_window, ovl_pattern, keep_mask, basis_values, rest_density,
    slab_owner, cell_lengths,
):
    return final_copy(main_call(
        density, dens_pattern, margin_window, ovl_pattern.T, keep_mask, basis_values,
        rest_density, slab_owner, cell_lengths,
    ))


def solution(mesh):
    return jax.shard_map(
        per_device,
        mesh=mesh,
        in_specs=(
            P("clus", "col"),
            P("clus", "col"),
            P("col", "clus"),
            P("col", "clus"),
            P("clus", "col"),
            P("col", None, None),
            P("clus", "col", None),
            P(),
            P(),
        ),
        out_specs=(P("clus", "col", None), P("clus", "col"), P("clus", "col")),
        check_vma=False,
    )
```

```python
import functools
import math

import jax
import jax.numpy as jnp
import ml_dtypes
import numpy as np
from jax import lax
from jax.experimental import pallas as pl
from jax.experimental.pallas import tpu as pltpu
from jax.sharding import PartitionSpec as P

B = 256
G = 256
QZ = 128
NX, NY, NZ = 4, 4, 4
ND = 128
CH = 128
NCH = 32
SHARE = (8, 4, 0, 4)
FIRST = (0, 8, 12, 12)
MOST = 8
ARRIVE = [FIRST[d] + i for i in range(MOST) for d in (0, 1, 3, 2) if i < SHARE[d]]
four_pi = 4.0 * math.pi
f32 = jnp.float32
bf16 = jnp.bfloat16
MESH = pl.DeviceIdType.MESH
NT = (((1,), (1,)), ((), ()))
TN = (((0,), (0,)), ((), ()))
NN = (((1,), (0,)), ((), ()))


def split_np(a):
    hi = a.astype(np.float32).astype(ml_dtypes.bfloat16)
    lo = (a - hi.astype(np.float64)).astype(np.float32).astype(ml_dtypes.bfloat16)
    return [hi, lo]


def x_of_row(row):
    return (row % 64) // 4 * 16 + row % 4 * 4 + row // 64


@functools.lru_cache(maxsize=1)
def tables():
    n = np.arange(G)
    ang = 2.0 * np.pi * (n[:, None] * n[None, :] % G) / G
    cos, sin = np.cos(ang), np.sin(ang)
    half = cos[:128], sin[:128]
    tz = np.concatenate([half[0], -half[1]], 0)
    tz[128] = cos[128]
    tzi = np.concatenate([2.0 * half[0], -2.0 * half[1]], 0)
    tzi[0] = 1.0
    tzi[128] = cos[128]
    tzi = tzi / float(G) ** 3
    perm = x_of_row(n)
    wx = np.concatenate([cos[:, perm], sin[:, perm]], 0)
    wi = np.concatenate([cos[perm], sin[perm]], 0)
    tq = np.concatenate([tz[:128, 64:192], tz[128:, 64:192]], 1)
    kc = np.arange(ND) % 16 * 8 + np.arange(ND) // 16
    tzi = np.concatenate([tzi[:128][kc], tzi[128:][kc]], 0)
    tp = np.concatenate([tzi[:128, 64:192], tzi[128:, 64:192]], 1)
    t1 = np.concatenate(sum([split_np(a) for a in (tz, tzi, wx, wi, tp, tq)], []), 0)
    ty = np.concatenate(split_np(np.concatenate([cos, sin], 1)), 0)
    row = np.arange(1024)
    ri, il, y = row // 512, row // 256 % 2, row % 256
    lane = ri * 64 + il * 32 + y // 32 * 4 + y % 4
    sel_c = (lane[:, None] == np.arange(128)[None, :]) & (y % 32 < 8)[:, None]
    sel_c = sel_c.astype(np.float32).astype(ml_dtypes.bfloat16)
    return t1, ty, sel_c


ROWS = {}
at = 0
for name, rows in (
    ("tz", 256), ("tzi", 256), ("wx", 512), ("wi", 512), ("tp", 128), ("tq", 128)
):
    ROWS[name] = (at, rows)
    at += 2 * rows
T1_ROWS = at


def split2(a):
    hi = a.astype(bf16)
    lo = (a - hi.astype(f32)).astype(bf16)
    return hi, lo


def dot(a, b, dims=NN):
    return lax.dot_general(a, b, dims, preferred_element_type=f32)


def dot3(a, b, dims=NN):
    return dot(a[0], b[0], dims) + (dot(a[0], b[1], dims) + dot(a[1], b[0], dims))


def kernel(
    pat_ref, len_ref, ovl_ref, keep_ref, margin_ref, own_ref, dens_ref, phi_ref, rest_ref,
    t1_hbm, ty_hbm, selc_hbm,
    pot_out, har_out, prod_out,
    pot_ref, har_ref, prod_ref,
    phi, rblk, relay, masked, wt, t1, ty, selc,
    s1, x1, r1, s2, x2, r2, s3, x3, r3, v1, xv, rv, rp, rq, pad, xa, ga, gb, big,
    wd, wm, tt, trx, zs, zr, ys, yr,
    lsem, tsem, rsem, ssem, fsem, q_s, q_r,
    a1_s, a1_r, a2_s, a2_r, g1_s, g1_r, g2_s, g2_r, p1_s, p1_r, p2_s, p2_r, b1_s, b1_r, b2_s, b2_r,
    wd_s, wd_r, wm_s, wm_r, tw_s, tw_r, zs_s, zr_r, ys_s, yr_r, osem,
):
    c = lax.axis_index("clus")
    k = lax.axis_index("col")
    me = c * 8 + k
    x, y = c // 4, c % 4
    z, h = k // 2, k % 2
    zp, zm, z2 = (z + 1) % 4, (z + 3) % 4, (z + 2) % 4
    root = h == y // 2
    hub = x == z
    far = jnp.logical_not(hub)
    twin = (c, z * 2 + 1 - h)

    def part(name, lo):
        first, rows = ROWS[name]
        return t1[pl.ds(first + lo * rows, rows), :]

    def table(name):
        return part(name, 0), part(name, 1)

    def local(src, dst, sem):
        return pltpu.make_async_copy(src, dst, sem)

    def remote(src, dst, send, recv, to):
        return pltpu.make_async_remote_copy(
            src_ref=src, dst_ref=dst, send_sem=send, recv_sem=recv, device_id=to, device_id_type=MESH
        )

    def clus_group(src_of, dst, send_sem, recv_sem):
        def body(i, carry):
            to = lax.rem(c + i, 16)
            remote(src_of(to), dst.at[c], send_sem, recv_sem, (to, k)).start()
            return carry

        lax.fori_loop(1, 16, body, 0)
        local(src_of(c), dst.at[c], recv_sem).start()

    def col_group(src_of, dst, send_sem, recv_sem):
        for i in range(1, 8):
            to = (k + i) % 8
            remote(src_of(to), dst.at[k], send_sem, recv_sem, (c, to)).start()
        local(src_of(k), dst.at[k], recv_sem).start()

    bar = pltpu.get_barrier_semaphore()

    def greet(i, carry):
        pl.semaphore_signal(bar, inc=1, device_id=(lax.rem(c + i, 16), k), device_id_type=MESH)
        return carry

    lax.fori_loop(1, 16, greet, 0)
    for i in range(1, 8):
        pl.semaphore_signal(bar, inc=1, device_id=(c, (k + i) % 8), device_id_type=MESH)
    loads = [
        local(t1_hbm, t1, lsem.at[0]),
        local(phi_ref, phi, lsem.at[1]),
        local(ty_hbm, ty, lsem.at[2]),
        local(selc_hbm, selc, lsem.at[3]),
    ]
    for copy in loads:
        copy.start()
    pl.semaphore_wait(bar, 22)

    first = 2 * (y % 2)

    def own_part(g):
        return phi_ref.at[pl.ds(first, 2), :, pl.ds(pl.multiple_of(g * CH, CH), CH)]

    to_send = []

    def send(when, src, dst, recv, to):
        index = len(to_send)
        copy = remote(src, dst, ssem.at[index], recv, to)
        to_send.append((when, copy))
        pl.when(when)(copy.start)

    def share(dist):
        pair, count = FIRST[0], SHARE[0]
        for d in range(1, 4):
            pair = jnp.where(dist == d, FIRST[d], pair)
            count = jnp.where(dist == d, SHARE[d], count)
        return pair, count

    my_pair, my_count = share((x - z) % 4)

    def batch(i):
        for turn in range(2):
            for up in (True, False):
                half = turn if up else 1 - turn
                slot = 0 if up else 1
                send(
                    root & (i < my_count), own_part(jnp.minimum(2 * (my_pair + i) + half, NCH - 1)),
                    relay.at[slot, i], tsem.at[slot, i], (c, (zp if up else zm) * 2 + half),
                )

    batch(0)
    batch(1)

    for i in range(2):
        for j in range(4):
            keep = pat_ref[i, j].astype(f32).astype(bf16)
            at_rows, at_cols = pl.ds(i * B, B), pl.ds(j * B, B)
            masked[at_rows, at_cols] = dens_ref[at_rows, at_cols] * keep
    wd[y] = masked[0:B, :]
    for j in range(4):
        at_rows = pl.ds(j * B, B)
        wm[x, at_rows, :] = margin_ref[at_rows, :] * ovl_ref[0, j].astype(f32).astype(bf16)
    to_y = [(x * 4 + (y + i) % 4, k) for i in range(1, 4)]
    to_x = [((x + i) % 4 * 4 + y, k) for i in range(1, 4)]
    rows_out = [remote(wd.at[y], wd.at[y], wd_s.at[i], wd_r.at[y], to) for i, to in enumerate(to_y)]
    cols_out = [remote(wm.at[x], wm.at[x], wm_s.at[i], wm_r.at[x], to) for i, to in enumerate(to_x)]
    for copy in rows_out:
        copy.start()

    loads[0].wait()
    lines = dot3(table("tz"), split2(rest_ref[...].reshape(512, G)), NT)
    for i in range(2):
        for j in range(4):
            s1[:, i * 4 + j, :] = lines[i * 128 : (i + 1) * 128, j * 128 : (j + 1) * 128]
    clus_group(lambda to: s1.at[pl.ds(pl.multiple_of(to * 8, 8), 8)], x1, a1_s, a1_r)
    for copy in cols_out:
        copy.start()

    hub_root = hub & root

    @pl.when(hub_root)
    def _():
        def body(g, carry):
            remote(own_part(g), rblk.at[g], fsem.at[g], rsem.at[g], twin).start()
            local(own_part(g), rblk.at[g], rsem.at[g]).start()
            return carry

        lax.fori_loop(0, NCH, body, 0)

    row_id = lax.broadcasted_iota(jnp.int32, (G, G), 0)
    col_id = lax.broadcasted_iota(jnp.int32, (G, G), 1)

    def wave(freq, axis):
        signed = jnp.where(freq < G // 2, freq, freq - G).astype(f32)
        scaled = signed * (2.0 * math.pi) / jnp.full(freq.shape, len_ref[axis], f32)
        return scaled * scaled

    flat = wave(row_id, 0) + wave(col_id, 1)
    for out, kz in ((ga, me), (gb, jnp.where(me == 0, 128, me))):
        kz = jnp.full((G, G), kz, jnp.int32)
        anchor = (row_id == 0) & (col_id == 0) & (kz == 0)
        out[...] = jnp.where(anchor, 0.0, four_pi / jnp.where(anchor, 1.0, flat + wave(kz, 2)))

    loads[1].wait()
    stages = []
    for i in range(MOST + 1):
        if i < MOST:
            stages += [(0, i), (1, i)]
        if i:
            stages.append((2, i - 1))
    for slot, i in stages:
        plane = (zm, zp, z2)[slot]
        pair, count = share((x - plane) % 4)
        have = i < count

        @pl.when(have)
        def _():
            local(relay.at[slot, i], relay.at[slot, i], tsem.at[slot, i]).wait()

        if slot == 1 and i + 2 < MOST:
            batch(i + 2)
        if slot == 0:
            send(have & (h == 0), relay.at[0, i], relay.at[2, i], tsem.at[2, i], (c, zp * 2))
        if slot == 1:
            send(have & (h == 1), relay.at[1, i], relay.at[2, i], tsem.at[2, i], (c, zm * 2 + 1))
        here = plane == x
        g = jnp.minimum(2 * (pair + i) + h, NCH - 1)
        send(have & here, relay.at[slot, i], rblk.at[g], rsem.at[g], twin)
        send(have & jnp.logical_not(here), relay.at[slot, i], rblk.at[g], rsem.at[g], (plane * 4 + y, k))

        @pl.when(have & here)
        def _():
            local(relay.at[slot, i], rblk.at[g], rsem.at[g]).start()

    local(x1, x1, a1_r).wait()
    col_group(lambda to: x1.at[:, to], r1, a2_s, a2_r)

    def block_of(row):
        return row % 16 * 2 + row // 16

    spot = lax.broadcasted_iota(jnp.int32, (1, 32), 1)
    x_cell = jnp.zeros((1, 32), jnp.int32)
    order = lax.broadcasted_iota(jnp.int32, (32, G), 0)
    x_pick = jnp.zeros((32, G), jnp.int32)
    for row in range(32):
        cell = own_ref[block_of(row)] * 16 + block_of(row) % 16
        x_cell = jnp.where(spot == row, cell, x_cell)
        x_pick = jnp.where(order == row, cell, x_pick)
    row_x = x_of_row(lax.broadcasted_iota(jnp.int32, (G, 1), 0))
    sits = (row_x == x_cell).astype(f32).astype(bf16)
    row_of = x_of_row(lax.broadcasted_iota(jnp.int32, (32, G), 1))
    pick = (row_of == x_pick).astype(f32).astype(bf16)

    def pair_at(t):
        pair = ARRIVE[0]
        for i in range(1, 16):
            pair = jnp.where(t == i, ARRIVE[i], pair)
        return pair

    def passed_on(pair):
        g = 2 * pair + h
        return far & (pair >= SHARE[0]), remote(rblk.at[g], rblk.at[g], fsem.at[g], rsem.at[g], twin)

    def step(t, carry):
        @pl.when(t < 16)
        def _():
            pair = pair_at(t)
            g = 2 * pair + h
            local(rblk.at[g], rblk.at[g], rsem.at[g]).wait()
            when, copy = passed_on(pair)
            pl.when(when)(copy.start)

        @pl.when(t > 0)
        def _():
            pair = pair_at(t - 1)
            g = 2 * pair + 1 - h
            local(rblk.at[g], rblk.at[g], rsem.at[g]).wait()
            cells = pl.ds(pl.multiple_of(pair * 2 * CH, 2 * CH), 2 * CH)
            values = phi[:, :, cells].reshape(4 * B, 2 * CH)
            for i in range(2):
                lifted = dot(masked[i * B : (i + 1) * B, :], values)
                for j in range(2):
                    basis = rblk[2 * pair + j, i].astype(f32)
                    summed = jnp.sum(basis * lifted[:, j * CH : (j + 1) * CH], axis=0, keepdims=True)
                    rp[pair // 2, pl.ds(i * 4 + pair % 2 * 2 + j, 1), :] = summed

        return carry

    lax.fori_loop(0, 17, step, 0)
    for l in range(8):
        away = l != k

        @pl.when(away)
        def _():
            remote(rp.at[l], rq.at[k], q_s.at[l], q_r.at[k], (c, l)).start()

        @pl.when(jnp.logical_not(away))
        def _():
            local(rp.at[l], rq.at[k], q_r.at[k]).start()

    for i in range(1, 4):
        ny, nx = (y + i) % 4, (x + i) % 4
        local(wd.at[ny], wd.at[ny], wd_r.at[ny]).wait()
        local(wm.at[nx], wm.at[nx], wm_r.at[nx]).wait()

    def tile_step(t, carry):
        tt[t % 4 // 2, t // 4, t % 2] = dot(wd[t // 4], wm[t % 4])
        return carry

    lax.fori_loop(0, 16, tile_step, 0)
    swap = remote(tt.at[1 - h], trx, tw_s, tw_r, twin)
    swap.start()
    for l in range(8):
        local(rq.at[l], rq.at[l], q_r.at[l]).wait()
    rho = jnp.sum(rq[...], axis=0)

    pad[...] = jnp.zeros_like(pad)
    pad[0:8, 0:128] = rho
    pad[8:16, 128:256] = rho
    for copy in loads[2:]:
        copy.wait()
    v1[...] = dot3(table("tq"), split2(pad[...]), NT).reshape(ND, 1, 128)
    clus_group(lambda to: v1.at[pl.ds(to * 8, 8)], xv, g1_s, g1_r)

    local(xv, xv, g1_r).wait()
    col_group(lambda to: xv.at[:, to], rv, g2_s, g2_r)

    lane = lax.broadcasted_iota(jnp.int32, (1, 1, 128), 2) // 32
    low = lax.broadcasted_iota(jnp.int32, (1, 8, 1), 1) < 4
    local(r1, r1, a2_r).wait()
    for kk in range(2):
        got = [r1[kk * 4 + k4] for k4 in range(4)]
        for p4 in range(4):
            tile = got[p4]
            for k4 in range(4):
                if k4 != p4:
                    turned = pltpu.roll(got[k4], (k4 - p4) % 4 * 32, 2)
                    tile = jnp.where(lane == k4, turned, tile)
            pairs = tile.reshape(8, 2, 8, 128)
            even, odd = pairs[:, 0], pairs[:, 1]
            at_rows, at_cols = pl.ds(p4 * 64, 64), pl.ds(kk * 128, 128)
            xa[at_rows, at_cols] = jnp.where(low, even, pltpu.roll(odd, 4, 1)).reshape(64, 128)
            xa[pl.ds(256 + p4 * 64, 64), at_cols] = jnp.where(low, pltpu.roll(even, 4, 1), odd).reshape(64, 128)

    lane_id = lax.broadcasted_iota(jnp.int32, (16, 128), 1)
    upper = lax.broadcasted_iota(jnp.int32, (16, 128), 0) // 8
    valid_lane = lane_id % 32 // 4 == upper
    ty_pair = ty[0:G, :], ty[G : 2 * G, :]
    wx, wi = table("wx"), table("wi")

    def spectrum(tab, lines):
        parts = []
        for values in lines:
            quad = dot3(tab, split2(values))
            parts.append((quad[:G, :G] - quad[G:, G:], -(quad[G:, :G] + quad[:G, G:])))
        (a_re, a_im), (b_re, b_im) = parts
        return ga[...] * a_re - gb[...] * b_im, ga[...] * a_im + gb[...] * b_re

    big[...] = dot3(split2(xa[...]), ty_pair)
    xa[0:G, :], xa[G : 2 * G, :] = spectrum(wx, (big[0:G, :], big[G : 2 * G, :]))
    at_x = tuple(dot(tab, sits).astype(bf16) for tab in wx)
    to_x_rows = tuple(
        jnp.concatenate([dot(pick, tab[:G]), dot(pick, tab[G:])], axis=0).astype(bf16) for tab in wi
    )

    swap.wait_recv()
    side = y // 2

    def to_collect(i):
        target = 2 * h + i
        stays = (target == z) & (side == h)
        return stays, remote(zs.at[i], zr.at[z], zs_s.at[i], zr_r.at[z], (c, target * 2 + side))

    for i in range(2):
        for j in range(4):
            zs[i, j] = (tt[h, j, i] + trx[j, i]).astype(bf16)
        stays, copy = to_collect(i)
        pl.when(jnp.logical_not(stays))(copy.start)

        @pl.when(stays)
        def _():
            local(zs.at[i], zr.at[z], zr_r.at[z]).start()

    local(rv, rv, g2_r).wait()
    spread = []
    for half in range(2):
        acc = None
        for l4 in range(4):
            values = rv[half * 4 + l4].reshape(16, 128)
            if l4:
                values = pltpu.roll(values, l4 * 32, 1)
            acc = values if acc is None else jnp.where(lane_id // 32 == l4, values, acc)
        spread.append(acc)
    lines_y = []
    for i in range(2):
        rows = []
        for il in range(2):
            offset = i * 8 + il * 4
            halves = []
            for acc in spread:
                low_row = pltpu.roll(acc, (128 - offset) % 128, 1) if offset else acc
                high_row = pltpu.roll(acc, (132 - offset) % 128, 1) if offset != 4 else acc
                halves.append(jnp.where(valid_lane, jnp.where(upper == 0, low_row, high_row), 0.0))
            rows.append(jnp.concatenate(halves, axis=1))
        lines_y.append(jnp.concatenate(rows, axis=0))

    patch_y = dot3(split2(jnp.concatenate(lines_y, axis=0)), ty_pair)
    p_re, p_im = spectrum(at_x, (patch_y[:32], patch_y[32:]))
    p_re, p_im = xa[0:G, :] + p_re, xa[G : 2 * G, :] + p_im
    xa[0:G, :] = p_re
    xa[G : 2 * G, :] = p_im

    from_re, from_im = dot3(to_x_rows, split2(p_re)), dot3(to_x_rows, split2(p_im))
    t_re, t_im = from_re[:32] - from_im[32:], from_im[:32] + from_re[32:]
    back = dot3(split2(jnp.concatenate([t_re, t_im], axis=0)), ty_pair)
    on_patch = back[:32, :G] - back[32:, G:], back[:32, G:] + back[32:, :G]
    line = lax.broadcasted_iota(jnp.int32, (32, G), 1)
    valid = line % 32 // 4 == order % 16 // 8
    rows = []
    for i in range(2):
        here = jnp.where(valid, on_patch[i], 0.0)
        rows += [here[0:16], here[16:32]]
    hi, lo = split2(jnp.concatenate(rows, axis=1))
    packed = dot(hi, selc[...]) + dot(lo, selc[...])
    for i in range(16):
        s3[i] = packed[i : i + 1, :]
    clus_group(lambda to: s3.at[to], x3, p1_s, p1_r)

    back = dot3(split2(xa[...]), ty_pair)
    local(x3, x3, p1_r).wait()
    col_group(lambda to: x3, r3, p2_s, p2_r)
    big[0:G, 0:G] = back[:G, :G] - back[G:, G:]
    big[0:G, G : 2 * G] = back[:G, G:] + back[G:, :G]
    quad = dot3(wi, split2(big[0:G, :]))
    xa[0:G, :] = quad[:G, :G] - quad[G:, G:]
    xa[G : 2 * G, :] = quad[:G, G:] + quad[G:, :G]
    for kk in range(2):
        tiles = []
        at_cols = pl.ds(kk * 128, 128)
        for p4 in range(4):
            re = xa[pl.ds(p4 * 64, 64), at_cols].reshape(8, 8, 128)
            im = xa[pl.ds(256 + p4 * 64, 64), at_cols].reshape(8, 8, 128)
            even = jnp.where(low, re, pltpu.roll(im, 4, 1))
            odd = jnp.where(low, pltpu.roll(re, 4, 1), im)
            tiles.append(jnp.stack([even, odd], axis=1).reshape(16, 8, 128))
        for k4 in range(4):
            tile = tiles[k4]
            for p4 in range(4):
                if p4 != k4:
                    tile = jnp.where(lane == p4, pltpu.roll(tiles[p4], (p4 - k4) % 4 * 32, 2), tile)
            s2[:, kk * 4 + k4] = tile
    clus_group(lambda to: s2.at[to], x2, b1_s, b1_r)
    collects = h == side

    def to_owner(j):
        ny = (y + j) % 4
        return remote(ys.at[ny], yr.at[y % 2], ys_s.at[j - 1], yr_r.at[y % 2], (x * 4 + ny, k))

    @pl.when(collects)
    def _():
        for i in range(4):
            local(zr.at[i], zr.at[i], zr_r.at[i]).wait()
        for j in range(4):
            total = zr[0, j].astype(f32) + zr[1, j].astype(f32) + (zr[2, j].astype(f32) + zr[3, j].astype(f32))
            ys[j] = total.astype(bf16)
        for j in range(1, 4):
            to_owner(j).start()
        local(ys.at[y], yr.at[y % 2], yr_r.at[y % 2]).start()

    local(r3, r3, p2_r).wait()
    arrived = split2(r3[...].reshape(ND, 128))
    both = dot3(arrived, table("tp"), TN)
    rho_pot = both[:64, :128] + both[64:, 128:]
    for i in range(2):
        for g in range(NCH):
            at_row = i * 32 + g
            scaled = rblk[g, i].astype(f32) * rho_pot[at_row : at_row + 1, :]
            wt[pl.ds(i * B, B), pl.ds(g * CH, CH)] = scaled.astype(bf16)
    for j in range(4):
        if j == 2:
            local(x2, x2, b1_r).wait()
            col_group(lambda to: x2.at[:, to], r2, b2_s, b2_r)
        for i in range(2):
            block_sum = dot(wt[pl.ds(i * B, B), :], phi[j], NT)
            har_ref[pl.ds(i * B, B), pl.ds(j * B, B)] = (block_sum * pat_ref[i, j].astype(f32)).astype(bf16)

    done = [local(har_ref, har_out, osem.at[0])]
    done[0].start()
    local(r2, r2, b2_r).wait()
    lines_back = r2[...].reshape(ND, 8, 128)
    tzi = table("tzi")
    for j in range(4):
        got = jnp.concatenate([lines_back[:, j, :], lines_back[:, 4 + j, :]], axis=0)
        pot_ref[pl.ds(j * 4, 4)] = dot3(split2(got), tzi, TN).reshape(4, 32, G)

    done.append(local(pot_ref, pot_out, osem.at[1]))
    done[1].start()
    for i in range(2):
        local(yr.at[i], yr.at[i], yr_r.at[i]).wait()
        prod_ref[:, pl.ds(i * B, B)] = yr[i] * keep_ref[0, i].astype(f32).astype(bf16)

    done.append(local(prod_ref, prod_out, osem.at[2]))
    done[2].start()

    for copy in rows_out + cols_out + [swap]:
        copy.wait_send()
    for i in range(2):
        stays, copy = to_collect(i)
        pl.when(jnp.logical_not(stays))(copy.wait_send)

    @pl.when(collects)
    def _():
        for j in range(1, 4):
            to_owner(j).wait_send()

    for when, copy in to_send:
        pl.when(when)(copy.wait_send)

    def leave(g, carry):
        remote(rblk.at[g], rblk.at[g], fsem.at[g], rsem.at[g], twin).wait_send()
        return carry

    @pl.when(hub_root)
    def _():
        lax.fori_loop(0, NCH, leave, 0)

    @pl.when(far)
    def _():
        lax.fori_loop(SHARE[0], 16, lambda pair, carry: leave(2 * pair + h, carry), 0)

    for l in range(8):

        @pl.when(l != k)
        def _():
            remote(rp.at[l], rq.at[k], q_s.at[l], q_r.at[k], (c, l)).wait_send()

    for dst, sem in ((x1, a1_s), (xv, g1_s), (x3, p1_s), (x2, b1_s)):
        rest_of = dst.at[pl.ds(0, 15)]
        local(rest_of, rest_of, sem).wait()
    for dst, sem in ((r1, a2_s), (rv, g2_s), (r3, p2_s), (r2, b2_s)):
        rest_of = dst.at[pl.ds(0, 7)]
        local(rest_of, rest_of, sem).wait()
    for copy in done:
        copy.wait()


def hand_over(*refs):
    arrays, outs, held, sem = refs[:3], refs[3:6], refs[6:9], refs[9]
    into = [pltpu.make_async_copy(arrays[i], held[i], sem.at[i]) for i in range(3)]
    away = [pltpu.make_async_copy(held[i], outs[i], sem.at[3 + i]) for i in range(3)]
    for copy in into:
        copy.start()
    for i in (2, 0, 1):
        into[i].wait()
        away[i].start()
    for copy in away:
        copy.wait()


def final_copy(arrays):
    hbm = pl.BlockSpec(memory_space=pl.ANY)
    return pl.pallas_call(
        hand_over,
        out_shape=tuple(jax.ShapeDtypeStruct(a.shape, a.dtype) for a in arrays),
        in_specs=[hbm] * 3,
        out_specs=(hbm,) * 3,
        scratch_shapes=[pltpu.VMEM(a.shape, a.dtype) for a in arrays] + [pltpu.SemaphoreType.DMA((6,))],
        compiler_params=pltpu.CompilerParams(vmem_limit_bytes=62 << 20),
        cost_estimate=pl.CostEstimate(flops=0, bytes_accessed=4 << 20, transcendentals=0),
    )(*arrays)


def main_call(density, pattern, margin, ovl, keep, basis, rest, slab_owner, lengths):
    t1, ty, selc = tables()
    vmem = pl.BlockSpec(memory_space=pltpu.VMEM)
    smem = pl.BlockSpec(memory_space=pltpu.SMEM)
    hbm = pl.BlockSpec(memory_space=pl.ANY)
    V = pltpu.VMEM
    D = pltpu.SemaphoreType.DMA
    return pl.pallas_call(
        kernel,
        out_shape=(
            jax.ShapeDtypeStruct((16, 32, G), f32),
            jax.ShapeDtypeStruct((512, 1024), bf16),
            jax.ShapeDtypeStruct((B, 2 * B), bf16),
        ),
        in_specs=[smem] * 4 + [vmem, smem, vmem, hbm, vmem, hbm, hbm, hbm],
        out_specs=(hbm, hbm, hbm),
        scratch_shapes=[
            V((16, 32, G), f32),
            V((512, 1024), bf16),
            V((B, 2 * B), bf16),
            V((4, B, 4096), bf16),
            V((NCH, 2, B, CH), bf16),
            V((3, MOST, 2, B, CH), bf16),
            V((512, 1024), bf16),
            V((512, 4096), bf16),
            V((T1_ROWS, G), bf16),
            V((2 * G, 2 * G), bf16),
            V((1024, 128), bf16),
            V((ND, 8, 128), f32),
            V((16, 8, 8, 128), f32),
            V((8, 16, 8, 128), f32),
            V((16, 8, 8, 128), f32),
            V((16, 8, 8, 128), f32),
            V((8, 16, 8, 128), f32),
            V((16, 1, 128), f32),
            V((16, 1, 128), f32),
            V((8, 16, 1, 128), f32),
            V((ND, 1, 128), f32),
            V((16, 8, 1, 128), f32),
            V((8, 16, 1, 128), f32),
            V((8, 8, 128), f32),
            V((8, 8, 128), f32),
            V((128, 2 * 128), f32),
            V((2 * G, G), f32),
            V((G, G), f32),
            V((G, G), f32),
            V((2 * G, 2 * G), f32),
            V((4, B, 1024), bf16),
            V((4, 1024, B), bf16),
            V((2, 4, 2, B, B), f32),
            V((4, 2, B, B), f32),
            V((2, 4, B, B), bf16),
            V((4, 4, B, B), bf16),
            V((4, B, B), bf16),
            V((2, B, B), bf16),
            D((5,)),
            D((3, MOST)),
            D((NCH,)),
            D((128,)),
            D((NCH,)),
            D((8,)),
            D((8,)),
            *([D(())] * 16),
            D((3,)),
            D((4,)),
            D((3,)),
            D((4,)),
            D(()),
            D(()),
            D((2,)),
            D((4,)),
            D((3,)),
            D((2,)),
            D((3,)),
        ],
        compiler_params=pltpu.CompilerParams(
            collective_id=0, has_side_effects=True, vmem_limit_bytes=58 << 20
        ),
        cost_estimate=pl.CostEstimate(flops=12 * 10**9, bytes_accessed=24 << 20, transcendentals=0),
    )(pattern, lengths, ovl, keep, margin, slab_owner, density, basis, rest, t1, ty, selc)


def per_device(
    density, dens_pattern, margin_window, ovl_pattern, keep_mask, basis_values, rest_density,
    slab_owner, cell_lengths,
):
    return final_copy(main_call(
        density, dens_pattern, margin_window, ovl_pattern.T, keep_mask, basis_values,
        rest_density, slab_owner, cell_lengths,
    ))


def solution(mesh):
    return jax.shard_map(
        per_device,
        mesh=mesh,
        in_specs=(
            P("clus", "col"),
            P("clus", "col"),
            P("col", "clus"),
            P("col", "clus"),
            P("clus", "col"),
            P("col", None, None),
            P("clus", "col", None),
            P(),
            P(),
        ),
        out_specs=(P("clus", "col", None), P("clus", "col"), P("clus", "col")),
        check_vma=False,
    )
```

```python
import functools
import math

import jax
import jax.numpy as jnp
import ml_dtypes
import numpy as np
from jax import lax
from jax.experimental import pallas as pl
from jax.experimental.pallas import tpu as pltpu
from jax.sharding import PartitionSpec as P

B = 256
G = 256
QZ = 128
NX, NY, NZ = 4, 4, 4
ND = 128
CH = 128
NCH = 32
SHARE = (8, 4, 0, 4)
FIRST = (0, 8, 12, 12)
MOST = 8
ARRIVE = [FIRST[d] + i for i in range(MOST) for d in (0, 1, 3, 2) if i < SHARE[d]]
four_pi = 4.0 * math.pi
f32 = jnp.float32
bf16 = jnp.bfloat16
MESH = pl.DeviceIdType.MESH
NT = (((1,), (1,)), ((), ()))
TN = (((0,), (0,)), ((), ()))
NN = (((1,), (0,)), ((), ()))


def split_np(a):
    hi = a.astype(np.float32).astype(ml_dtypes.bfloat16)
    lo = (a - hi.astype(np.float64)).astype(np.float32).astype(ml_dtypes.bfloat16)
    return [hi, lo]


def x_of_row(row):
    return (row % 64) // 4 * 16 + row % 4 * 4 + row // 64


@functools.lru_cache(maxsize=1)
def tables():
    n = np.arange(G)
    ang = 2.0 * np.pi * (n[:, None] * n[None, :] % G) / G
    cos, sin = np.cos(ang), np.sin(ang)
    half = cos[:128], sin[:128]
    tz = np.concatenate([half[0], -half[1]], 0)
    tz[128] = cos[128]
    tzi = np.concatenate([2.0 * half[0], -2.0 * half[1]], 0)
    tzi[0] = 1.0
    tzi[128] = cos[128]
    tzi = tzi / float(G) ** 3
    perm = x_of_row(n)
    wx = np.concatenate([cos[:, perm], sin[:, perm]], 0)
    wi = np.concatenate([cos[perm], sin[perm]], 0)
    tq = np.concatenate([tz[:128, 64:192], tz[128:, 64:192]], 1)
    kc = np.arange(ND) % 16 * 8 + np.arange(ND) // 16
    tzi = np.concatenate([tzi[:128][kc], tzi[128:][kc]], 0)
    tp = np.concatenate([tzi[:128, 64:192], tzi[128:, 64:192]], 1)
    t1 = np.concatenate(sum([split_np(a) for a in (tz, tzi, wx, wi, tp, tq)], []), 0)
    ty = np.concatenate(split_np(np.concatenate([cos, sin], 1)), 0)
    row = np.arange(1024)
    ri, il, y = row // 512, row // 256 % 2, row % 256
    lane = ri * 64 + il * 32 + y // 32 * 4 + y % 4
    sel_c = (lane[:, None] == np.arange(128)[None, :]) & (y % 32 < 8)[:, None]
    sel_c = sel_c.astype(np.float32).astype(ml_dtypes.bfloat16)
    return t1, ty, sel_c


ROWS = {}
at = 0
for name, rows in (
    ("tz", 256), ("tzi", 256), ("wx", 512), ("wi", 512), ("tp", 128), ("tq", 128)
):
    ROWS[name] = (at, rows)
    at += 2 * rows
T1_ROWS = at


def split2(a):
    hi = a.astype(bf16)
    lo = (a - hi.astype(f32)).astype(bf16)
    return hi, lo


def dot(a, b, dims=NN):
    return lax.dot_general(a, b, dims, preferred_element_type=f32)


def dot3(a, b, dims=NN):
    return dot(a[0], b[0], dims) + (dot(a[0], b[1], dims) + dot(a[1], b[0], dims))


def kernel(
    pat_ref, len_ref, ovl_ref, keep_ref, margin_ref, own_ref, dens_ref, phi_ref, rest_ref,
    t1_hbm, ty_hbm, selc_hbm,
    pot_out, har_out, prod_out,
    pot_ref, har_ref, prod_ref,
    phi, rblk, relay, masked, wt, t1, ty, selc,
    s1, x1, r1, s2, x2, r2, s3, x3, r3, v1, xv, rv, rp, rq, pad, xa, ga, gb, big,
    wd, wm, tt, trx, zs, zr, ys, yr,
    lsem, tsem, rsem, ssem, fsem, q_s, q_r,
    a1_s, a1_r, a2_s, a2_r, g1_s, g1_r, g2_s, g2_r, p1_s, p1_r, p2_s, p2_r, b1_s, b1_r, b2_s, b2_r,
    wd_s, wd_r, wm_s, wm_r, tw_s, tw_r, zs_s, zr_r, ys_s, yr_r, osem,
):
    c = lax.axis_index("clus")
    k = lax.axis_index("col")
    me = c * 8 + k
    x, y = c // 4, c % 4
    z, h = k // 2, k % 2
    zp, zm, z2 = (z + 1) % 4, (z + 3) % 4, (z + 2) % 4
    root = h == y // 2
    hub = x == z
    far = jnp.logical_not(hub)
    twin = (c, z * 2 + 1 - h)

    def part(name, lo):
        first, rows = ROWS[name]
        return t1[pl.ds(first + lo * rows, rows), :]

    def table(name):
        return part(name, 0), part(name, 1)

    def local(src, dst, sem):
        return pltpu.make_async_copy(src, dst, sem)

    def remote(src, dst, send, recv, to):
        return pltpu.make_async_remote_copy(
            src_ref=src, dst_ref=dst, send_sem=send, recv_sem=recv, device_id=to, device_id_type=MESH
        )

    def clus_group(src_of, dst, send_sem, recv_sem):
        def body(i, carry):
            to = lax.rem(c + i, 16)
            remote(src_of(to), dst.at[c], send_sem, recv_sem, (to, k)).start()
            return carry

        lax.fori_loop(1, 16, body, 0)
        local(src_of(c), dst.at[c], recv_sem).start()

    def col_group(src_of, dst, send_sem, recv_sem):
        for i in range(1, 8):
            to = (k + i) % 8
            remote(src_of(to), dst.at[k], send_sem, recv_sem, (c, to)).start()
        local(src_of(k), dst.at[k], recv_sem).start()

    bar = pltpu.get_barrier_semaphore()

    def greet(i, carry):
        pl.semaphore_signal(bar, inc=1, device_id=(lax.rem(c + i, 16), k), device_id_type=MESH)
        return carry

    lax.fori_loop(1, 16, greet, 0)
    for i in range(1, 8):
        pl.semaphore_signal(bar, inc=1, device_id=(c, (k + i) % 8), device_id_type=MESH)
    loads = [
        local(t1_hbm, t1, lsem.at[0]),
        local(phi_ref, phi, lsem.at[1]),
        local(ty_hbm, ty, lsem.at[2]),
        local(selc_hbm, selc, lsem.at[3]),
    ]
    for copy in loads:
        copy.start()
    pl.semaphore_wait(bar, 22)

    first = 2 * (y % 2)

    def own_part(g):
        return phi_ref.at[pl.ds(first, 2), :, pl.ds(pl.multiple_of(g * CH, CH), CH)]

    to_send = []

    def send(when, src, dst, recv, to):
        index = len(to_send)
        copy = remote(src, dst, ssem.at[index], recv, to)
        to_send.append((when, copy))
        pl.when(when)(copy.start)

    def share(dist):
        pair, count = FIRST[0], SHARE[0]
        for d in range(1, 4):
            pair = jnp.where(dist == d, FIRST[d], pair)
            count = jnp.where(dist == d, SHARE[d], count)
        return pair, count

    my_pair, my_count = share((x - z) % 4)

    def batch(i):
        for turn in range(2):
            for up in (True, False):
                half = turn if up else 1 - turn
                slot = 0 if up else 1
                send(
                    root & (i < my_count), own_part(jnp.minimum(2 * (my_pair + i) + half, NCH - 1)),
                    relay.at[slot, i], tsem.at[slot, i], (c, (zp if up else zm) * 2 + half),
                )

    batch(0)
    batch(1)

    for i in range(2):
        for j in range(4):
            keep = pat_ref[i, j].astype(f32).astype(bf16)
            at_rows, at_cols = pl.ds(i * B, B), pl.ds(j * B, B)
            masked[at_rows, at_cols] = dens_ref[at_rows, at_cols] * keep
    wd[y] = masked[0:B, :]
    for j in range(4):
        at_rows = pl.ds(j * B, B)
        wm[x, at_rows, :] = margin_ref[at_rows, :] * ovl_ref[0, j].astype(f32).astype(bf16)
    to_y = [(x * 4 + (y + i) % 4, k) for i in range(1, 4)]
    to_x = [((x + i) % 4 * 4 + y, k) for i in range(1, 4)]
    rows_out = [remote(wd.at[y], wd.at[y], wd_s.at[i], wd_r.at[y], to) for i, to in enumerate(to_y)]
    cols_out = [remote(wm.at[x], wm.at[x], wm_s.at[i], wm_r.at[x], to) for i, to in enumerate(to_x)]
    for copy in rows_out:
        copy.start()

    loads[0].wait()
    lines = dot3(table("tz"), split2(rest_ref[...].reshape(512, G)), NT)
    for i in range(2):
        for j in range(4):
            s1[:, i * 4 + j, :] = lines[i * 128 : (i + 1) * 128, j * 128 : (j + 1) * 128]
    clus_group(lambda to: s1.at[pl.ds(pl.multiple_of(to * 8, 8), 8)], x1, a1_s, a1_r)
    for copy in cols_out:
        copy.start()

    hub_root = hub & root

    @pl.when(hub_root)
    def _():
        def body(g, carry):
            remote(own_part(g), rblk.at[g], fsem.at[g], rsem.at[g], twin).start()
            local(own_part(g), rblk.at[g], rsem.at[g]).start()
            return carry

        lax.fori_loop(0, NCH, body, 0)

    row_id = lax.broadcasted_iota(jnp.int32, (G, G), 0)
    col_id = lax.broadcasted_iota(jnp.int32, (G, G), 1)

    def wave(freq, axis):
        signed = jnp.where(freq < G // 2, freq, freq - G).astype(f32)
        scaled = signed * (2.0 * math.pi) / jnp.full(freq.shape, len_ref[axis], f32)
        return scaled * scaled

    flat = wave(row_id, 0) + wave(col_id, 1)
    for out, kz in ((ga, me), (gb, jnp.where(me == 0, 128, me))):
        kz = jnp.full((G, G), kz, jnp.int32)
        anchor = (row_id == 0) & (col_id == 0) & (kz == 0)
        out[...] = jnp.where(anchor, 0.0, four_pi / jnp.where(anchor, 1.0, flat + wave(kz, 2)))

    loads[1].wait()
    stages = []
    for i in range(MOST + 1):
        if i < MOST:
            stages += [(0, i), (1, i)]
        if i:
            stages.append((2, i - 1))
    for slot, i in stages:
        plane = (zm, zp, z2)[slot]
        pair, count = share((x - plane) % 4)
        have = i < count

        @pl.when(have)
        def _():
            local(relay.at[slot, i], relay.at[slot, i], tsem.at[slot, i]).wait()

        if slot == 1 and i + 2 < MOST:
            batch(i + 2)
        if slot == 0:
            send(have & (h == 0), relay.at[0, i], relay.at[2, i], tsem.at[2, i], (c, zp * 2))
        if slot == 1:
            send(have & (h == 1), relay.at[1, i], relay.at[2, i], tsem.at[2, i], (c, zm * 2 + 1))
        here = plane == x
        g = jnp.minimum(2 * (pair + i) + h, NCH - 1)
        send(have & here, relay.at[slot, i], rblk.at[g], rsem.at[g], twin)
        send(have & jnp.logical_not(here), relay.at[slot, i], rblk.at[g], rsem.at[g], (plane * 4 + y, k))

        @pl.when(have & here)
        def _():
            local(relay.at[slot, i], rblk.at[g], rsem.at[g]).start()

    local(x1, x1, a1_r).wait()
    col_group(lambda to: x1.at[:, to], r1, a2_s, a2_r)

    def block_of(row):
        return row % 16 * 2 + row // 16

    spot = lax.broadcasted_iota(jnp.int32, (1, 32), 1)
    x_cell = jnp.zeros((1, 32), jnp.int32)
    order = lax.broadcasted_iota(jnp.int32, (32, G), 0)
    x_pick = jnp.zeros((32, G), jnp.int32)
    for row in range(32):
        cell = own_ref[block_of(row)] * 16 + block_of(row) % 16
        x_cell = jnp.where(spot == row, cell, x_cell)
        x_pick = jnp.where(order == row, cell, x_pick)
    row_x = x_of_row(lax.broadcasted_iota(jnp.int32, (G, 1), 0))
    sits = (row_x == x_cell).astype(f32).astype(bf16)
    row_of = x_of_row(lax.broadcasted_iota(jnp.int32, (32, G), 1))
    pick = (row_of == x_pick).astype(f32).astype(bf16)

    def pair_at(t):
        pair = ARRIVE[0]
        for i in range(1, 16):
            pair = jnp.where(t == i, ARRIVE[i], pair)
        return pair

    def passed_on(pair):
        g = 2 * pair + h
        return far & (pair >= SHARE[0]), remote(rblk.at[g], rblk.at[g], fsem.at[g], rsem.at[g], twin)

    def step(t, carry):
        @pl.when(t < 16)
        def _():
            pair = pair_at(t)
            g = 2 * pair + h
            local(rblk.at[g], rblk.at[g], rsem.at[g]).wait()
            when, copy = passed_on(pair)
            pl.when(when)(copy.start)

        @pl.when(t > 0)
        def _():
            pair = pair_at(t - 1)
            g = 2 * pair + 1 - h
            local(rblk.at[g], rblk.at[g], rsem.at[g]).wait()
            cells = pl.ds(pl.multiple_of(pair * 2 * CH, 2 * CH), 2 * CH)
            values = phi[:, :, cells].reshape(4 * B, 2 * CH)
            for i in range(2):
                lifted = dot(masked[i * B : (i + 1) * B, :], values)
                for j in range(2):
                    basis = rblk[2 * pair + j, i].astype(f32)
                    summed = jnp.sum(basis * lifted[:, j * CH : (j + 1) * CH], axis=0, keepdims=True)
                    rp[pair // 2, pl.ds(i * 4 + pair % 2 * 2 + j, 1), :] = summed

        return carry

    lax.fori_loop(0, 17, step, 0)
    for l in range(8):
        away = l != k

        @pl.when(away)
        def _():
            remote(rp.at[l], rq.at[k], q_s.at[l], q_r.at[k], (c, l)).start()

        @pl.when(jnp.logical_not(away))
        def _():
            local(rp.at[l], rq.at[k], q_r.at[k]).start()

    for i in range(1, 4):
        ny, nx = (y + i) % 4, (x + i) % 4
        local(wd.at[ny], wd.at[ny], wd_r.at[ny]).wait()
        local(wm.at[nx], wm.at[nx], wm_r.at[nx]).wait()

    def tile_step(t, carry):
        tt[t % 4 // 2, t // 4, t % 2] = dot(wd[t // 4], wm[t % 4])
        return carry

    lax.fori_loop(0, 16, tile_step, 0)
    swap = remote(tt.at[1 - h], trx, tw_s, tw_r, twin)
    swap.start()
    for l in range(8):
        local(rq.at[l], rq.at[l], q_r.at[l]).wait()
    rho = jnp.sum(rq[...], axis=0)

    pad[...] = jnp.zeros_like(pad)
    pad[0:8, 0:128] = rho
    pad[8:16, 128:256] = rho
    for copy in loads[2:]:
        copy.wait()
    v1[...] = dot3(table("tq"), split2(pad[...]), NT).reshape(ND, 1, 128)
    clus_group(lambda to: v1.at[pl.ds(to * 8, 8)], xv, g1_s, g1_r)

    local(xv, xv, g1_r).wait()
    col_group(lambda to: xv.at[:, to], rv, g2_s, g2_r)

    lane = lax.broadcasted_iota(jnp.int32, (1, 1, 128), 2) // 32
    low = lax.broadcasted_iota(jnp.int32, (1, 8, 1), 1) < 4
    local(r1, r1, a2_r).wait()
    for kk in range(2):
        got = [r1[kk * 4 + k4] for k4 in range(4)]
        for p4 in range(4):
            tile = got[p4]
            for k4 in range(4):
                if k4 != p4:
                    turned = pltpu.roll(got[k4], (k4 - p4) % 4 * 32, 2)
                    tile = jnp.where(lane == k4, turned, tile)
            pairs = tile.reshape(8, 2, 8, 128)
            even, odd = pairs[:, 0], pairs[:, 1]
            at_rows, at_cols = pl.ds(p4 * 64, 64), pl.ds(kk * 128, 128)
            xa[at_rows, at_cols] = jnp.where(low, even, pltpu.roll(odd, 4, 1)).reshape(64, 128)
            xa[pl.ds(256 + p4 * 64, 64), at_cols] = jnp.where(low, pltpu.roll(even, 4, 1), odd).reshape(64, 128)

    lane_id = lax.broadcasted_iota(jnp.int32, (16, 128), 1)
    upper = lax.broadcasted_iota(jnp.int32, (16, 128), 0) // 8
    valid_lane = lane_id % 32 // 4 == upper
    ty_pair = ty[0:G, :], ty[G : 2 * G, :]
    wx, wi = table("wx"), table("wi")

    def spectrum(tab, lines):
        parts = []
        for values in lines:
            quad = dot3(tab, split2(values))
            parts.append((quad[:G, :G] - quad[G:, G:], -(quad[G:, :G] + quad[:G, G:])))
        (a_re, a_im), (b_re, b_im) = parts
        return ga[...] * a_re - gb[...] * b_im, ga[...] * a_im + gb[...] * b_re

    big[...] = dot3(split2(xa[...]), ty_pair)
    xa[0:G, :], xa[G : 2 * G, :] = spectrum(wx, (big[0:G, :], big[G : 2 * G, :]))
    at_x = tuple(dot(tab, sits).astype(bf16) for tab in wx)
    to_x_rows = tuple(
        jnp.concatenate([dot(pick, tab[:G]), dot(pick, tab[G:])], axis=0).astype(bf16) for tab in wi
    )

    swap.wait_recv()
    side = y // 2

    def to_collect(i):
        target = 2 * h + i
        stays = (target == z) & (side == h)
        return stays, remote(zs.at[i], zr.at[z], zs_s.at[i], zr_r.at[z], (c, target * 2 + side))

    for i in range(2):
        for j in range(4):
            zs[i, j] = (tt[h, j, i] + trx[j, i]).astype(bf16)
        stays, copy = to_collect(i)
        pl.when(jnp.logical_not(stays))(copy.start)

        @pl.when(stays)
        def _():
            local(zs.at[i], zr.at[z], zr_r.at[z]).start()

    local(rv, rv, g2_r).wait()
    spread = []
    for half in range(2):
        acc = None
        for l4 in range(4):
            values = rv[half * 4 + l4].reshape(16, 128)
            if l4:
                values = pltpu.roll(values, l4 * 32, 1)
            acc = values if acc is None else jnp.where(lane_id // 32 == l4, values, acc)
        spread.append(acc)
    lines_y = []
    for i in range(2):
        rows = []
        for il in range(2):
            offset = i * 8 + il * 4
            halves = []
            for acc in spread:
                low_row = pltpu.roll(acc, (128 - offset) % 128, 1) if offset else acc
                high_row = pltpu.roll(acc, (132 - offset) % 128, 1) if offset != 4 else acc
                halves.append(jnp.where(valid_lane, jnp.where(upper == 0, low_row, high_row), 0.0))
            rows.append(jnp.concatenate(halves, axis=1))
        lines_y.append(jnp.concatenate(rows, axis=0))

    patch_y = dot3(split2(jnp.concatenate(lines_y, axis=0)), ty_pair)
    p_re, p_im = spectrum(at_x, (patch_y[:32], patch_y[32:]))
    p_re, p_im = xa[0:G, :] + p_re, xa[G : 2 * G, :] + p_im
    xa[0:G, :] = p_re
    xa[G : 2 * G, :] = p_im

    from_re, from_im = dot3(to_x_rows, split2(p_re)), dot3(to_x_rows, split2(p_im))
    t_re, t_im = from_re[:32] - from_im[32:], from_im[:32] + from_re[32:]
    back = dot3(split2(jnp.concatenate([t_re, t_im], axis=0)), ty_pair)
    on_patch = back[:32, :G] - back[32:, G:], back[:32, G:] + back[32:, :G]
    line = lax.broadcasted_iota(jnp.int32, (32, G), 1)
    valid = line % 32 // 4 == order % 16 // 8
    rows = []
    for i in range(2):
        here = jnp.where(valid, on_patch[i], 0.0)
        rows += [here[0:16], here[16:32]]
    hi, lo = split2(jnp.concatenate(rows, axis=1))
    packed = dot(hi, selc[...]) + dot(lo, selc[...])
    for i in range(16):
        s3[i] = packed[i : i + 1, :]
    clus_group(lambda to: s3.at[to], x3, p1_s, p1_r)

    back = dot3(split2(xa[...]), ty_pair)
    local(x3, x3, p1_r).wait()
    col_group(lambda to: x3, r3, p2_s, p2_r)
    big[0:G, 0:G] = back[:G, :G] - back[G:, G:]
    big[0:G, G : 2 * G] = back[:G, G:] + back[G:, :G]
    quad = dot3(wi, split2(big[0:G, :]))
    xa[0:G, :] = quad[:G, :G] - quad[G:, G:]
    xa[G : 2 * G, :] = quad[:G, G:] + quad[G:, :G]
    for kk in range(2):
        tiles = []
        at_cols = pl.ds(kk * 128, 128)
        for p4 in range(4):
            re = xa[pl.ds(p4 * 64, 64), at_cols].reshape(8, 8, 128)
            im = xa[pl.ds(256 + p4 * 64, 64), at_cols].reshape(8, 8, 128)
            even = jnp.where(low, re, pltpu.roll(im, 4, 1))
            odd = jnp.where(low, pltpu.roll(re, 4, 1), im)
            tiles.append(jnp.stack([even, odd], axis=1).reshape(16, 8, 128))
        for k4 in range(4):
            tile = tiles[k4]
            for p4 in range(4):
                if p4 != k4:
                    tile = jnp.where(lane == p4, pltpu.roll(tiles[p4], (p4 - k4) % 4 * 32, 2), tile)
            s2[:, kk * 4 + k4] = tile
    clus_group(lambda to: s2.at[to], x2, b1_s, b1_r)
    collects = h == side

    def to_owner(j):
        ny = (y + j) % 4
        return remote(ys.at[ny], yr.at[y % 2], ys_s.at[j - 1], yr_r.at[y % 2], (x * 4 + ny, k))

    @pl.when(collects)
    def _():
        for i in range(4):
            local(zr.at[i], zr.at[i], zr_r.at[i]).wait()
        for j in range(4):
            total = zr[0, j].astype(f32) + zr[1, j].astype(f32) + (zr[2, j].astype(f32) + zr[3, j].astype(f32))
            ys[j] = total.astype(bf16)
        for j in range(1, 4):
            to_owner(j).start()
        local(ys.at[y], yr.at[y % 2], yr_r.at[y % 2]).start()

    local(r3, r3, p2_r).wait()
    arrived = split2(r3[...].reshape(ND, 128))
    both = dot3(arrived, table("tp"), TN)
    rho_pot = both[:64, :128] + both[64:, 128:]
    for i in range(2):
        for g in range(NCH):
            at_row = i * 32 + g
            scaled = rblk[g, i].astype(f32) * rho_pot[at_row : at_row + 1, :]
            wt[pl.ds(i * B, B), pl.ds(g * CH, CH)] = scaled.astype(bf16)
    for j in range(4):
        if j == 2:
            local(x2, x2, b1_r).wait()
            col_group(lambda to: x2.at[:, to], r2, b2_s, b2_r)
        for i in range(2):
            block_sum = dot(wt[pl.ds(i * B, B), :], phi[j], NT)
            har_ref[pl.ds(i * B, B), pl.ds(j * B, B)] = (block_sum * pat_ref[i, j].astype(f32)).astype(bf16)

    done = [local(har_ref, har_out, osem.at[0])]
    done[0].start()
    local(r2, r2, b2_r).wait()
    lines_back = r2[...].reshape(ND, 8, 128)
    tzi = table("tzi")
    for j in range(4):
        got = jnp.concatenate([lines_back[:, j, :], lines_back[:, 4 + j, :]], axis=0)
        pot_ref[pl.ds(j * 4, 4)] = dot3(split2(got), tzi, TN).reshape(4, 32, G)

    done.append(local(pot_ref, pot_out, osem.at[1]))
    done[1].start()
    for i in range(2):
        local(yr.at[i], yr.at[i], yr_r.at[i]).wait()
        prod_ref[:, pl.ds(i * B, B)] = yr[i] * keep_ref[0, i].astype(f32).astype(bf16)

    done.append(local(prod_ref, prod_out, osem.at[2]))
    done[2].start()

    for copy in rows_out + cols_out + [swap]:
        copy.wait_send()
    for i in range(2):
        stays, copy = to_collect(i)
        pl.when(jnp.logical_not(stays))(copy.wait_send)

    @pl.when(collects)
    def _():
        for j in range(1, 4):
            to_owner(j).wait_send()

    for when, copy in to_send:
        pl.when(when)(copy.wait_send)

    def leave(g, carry):
        remote(rblk.at[g], rblk.at[g], fsem.at[g], rsem.at[g], twin).wait_send()
        return carry

    @pl.when(hub_root)
    def _():
        lax.fori_loop(0, NCH, leave, 0)

    @pl.when(far)
    def _():
        lax.fori_loop(SHARE[0], 16, lambda pair, carry: leave(2 * pair + h, carry), 0)

    for l in range(8):

        @pl.when(l != k)
        def _():
            remote(rp.at[l], rq.at[k], q_s.at[l], q_r.at[k], (c, l)).wait_send()

    for dst, sem in ((x1, a1_s), (xv, g1_s), (x3, p1_s), (x2, b1_s)):
        rest_of = dst.at[pl.ds(0, 15)]
        local(rest_of, rest_of, sem).wait()
    for dst, sem in ((r1, a2_s), (rv, g2_s), (r3, p2_s), (r2, b2_s)):
        rest_of = dst.at[pl.ds(0, 7)]
        local(rest_of, rest_of, sem).wait()
    for copy in done:
        copy.wait()


def hand_over(*refs):
    arrays, outs, held, sem = refs[:3], refs[3:6], refs[6:9], refs[9]
    into, away = [], []
    for piece in range(4):
        for i in range(3):
            rows = arrays[i].shape[0] // 4
            at_rows, index = pl.ds(piece * rows, rows), piece * 3 + i
            into.append(pltpu.make_async_copy(arrays[i].at[at_rows], held[i].at[at_rows], sem.at[index]))
            away.append(pltpu.make_async_copy(held[i].at[at_rows], outs[i].at[at_rows], sem.at[12 + index]))
    for copy in into:
        copy.start()
    for arrived, copy in zip(into, away):
        arrived.wait()
        copy.start()
    for copy in away:
        copy.wait()


def final_copy(arrays):
    hbm = pl.BlockSpec(memory_space=pl.ANY)
    return pl.pallas_call(
        hand_over,
        out_shape=tuple(jax.ShapeDtypeStruct(a.shape, a.dtype) for a in arrays),
        in_specs=[hbm] * 3,
        out_specs=(hbm,) * 3,
        scratch_shapes=[pltpu.VMEM(a.shape, a.dtype) for a in arrays] + [pltpu.SemaphoreType.DMA((24,))],
        compiler_params=pltpu.CompilerParams(vmem_limit_bytes=62 << 20),
        cost_estimate=pl.CostEstimate(flops=0, bytes_accessed=4 << 20, transcendentals=0),
    )(*arrays)


def main_call(density, pattern, margin, ovl, keep, basis, rest, slab_owner, lengths):
    t1, ty, selc = tables()
    vmem = pl.BlockSpec(memory_space=pltpu.VMEM)
    smem = pl.BlockSpec(memory_space=pltpu.SMEM)
    hbm = pl.BlockSpec(memory_space=pl.ANY)
    V = pltpu.VMEM
    D = pltpu.SemaphoreType.DMA
    return pl.pallas_call(
        kernel,
        out_shape=(
            jax.ShapeDtypeStruct((16, 32, G), f32),
            jax.ShapeDtypeStruct((512, 1024), bf16),
            jax.ShapeDtypeStruct((B, 2 * B), bf16),
        ),
        in_specs=[smem] * 4 + [vmem, smem, vmem, hbm, vmem, hbm, hbm, hbm],
        out_specs=(hbm, hbm, hbm),
        scratch_shapes=[
            V((16, 32, G), f32),
            V((512, 1024), bf16),
            V((B, 2 * B), bf16),
            V((4, B, 4096), bf16),
            V((NCH, 2, B, CH), bf16),
            V((3, MOST, 2, B, CH), bf16),
            V((512, 1024), bf16),
            V((512, 4096), bf16),
            V((T1_ROWS, G), bf16),
            V((2 * G, 2 * G), bf16),
            V((1024, 128), bf16),
            V((ND, 8, 128), f32),
            V((16, 8, 8, 128), f32),
            V((8, 16, 8, 128), f32),
            V((16, 8, 8, 128), f32),
            V((16, 8, 8, 128), f32),
            V((8, 16, 8, 128), f32),
            V((16, 1, 128), f32),
            V((16, 1, 128), f32),
            V((8, 16, 1, 128), f32),
            V((ND, 1, 128), f32),
            V((16, 8, 1, 128), f32),
            V((8, 16, 1, 128), f32),
            V((8, 8, 128), f32),
            V((8, 8, 128), f32),
            V((128, 2 * 128), f32),
            V((2 * G, G), f32),
            V((G, G), f32),
            V((G, G), f32),
            V((2 * G, 2 * G), f32),
            V((4, B, 1024), bf16),
            V((4, 1024, B), bf16),
            V((2, 4, 2, B, B), f32),
            V((4, 2, B, B), f32),
            V((2, 4, B, B), bf16),
            V((4, 4, B, B), bf16),
            V((4, B, B), bf16),
            V((2, B, B), bf16),
            D((5,)),
            D((3, MOST)),
            D((NCH,)),
            D((128,)),
            D((NCH,)),
            D((8,)),
            D((8,)),
            *([D(())] * 16),
            D((3,)),
            D((4,)),
            D((3,)),
            D((4,)),
            D(()),
            D(()),
            D((2,)),
            D((4,)),
            D((3,)),
            D((2,)),
            D((3,)),
        ],
        compiler_params=pltpu.CompilerParams(
            collective_id=0, has_side_effects=True, vmem_limit_bytes=58 << 20
        ),
        cost_estimate=pl.CostEstimate(flops=12 * 10**9, bytes_accessed=24 << 20, transcendentals=0),
    )(pattern, lengths, ovl, keep, margin, slab_owner, density, basis, rest, t1, ty, selc)


def per_device(
    density, dens_pattern, margin_window, ovl_pattern, keep_mask, basis_values, rest_density,
    slab_owner, cell_lengths,
):
    return final_copy(main_call(
        density, dens_pattern, margin_window, ovl_pattern.T, keep_mask, basis_values,
        rest_density, slab_owner, cell_lengths,
    ))


def solution(mesh):
    return jax.shard_map(
        per_device,
        mesh=mesh,
        in_specs=(
            P("clus", "col"),
            P("clus", "col"),
            P("col", "clus"),
            P("col", "clus"),
            P("clus", "col"),
            P("col", None, None),
            P("clus", "col", None),
            P(),
            P(),
        ),
        out_specs=(P("clus", "col", None), P("clus", "col"), P("clus", "col")),
        check_vma=False,
    )
```
